256 devices in a mesh: shot: 64 (over x, z, core), inline: 4 (over y).
Axes of the slice: x: 4, y: 4, z: 8, core: 2. Of those that a mesh axis runs over, the one named last changes fastest.
Arguments:
- traces: bfloat16 [262144, 2, 1536], P(('shot', 'inline')), may hold values from -6 to 6
- fold_bins: int32 [262144, 1], P(('shot', 'inline')), may hold values from 0 to 1023, as said below
- radii: int32 [12], replicated, may hold values from 1 to 8
Outputs:
- similarity: float32 [8, 512, 41, 1536], P('inline', 'shot')
The draws below stay inside these ranges and needn't reach their ends.
Inputs may be any that keep to these rules, and one draw needn't show every extreme that they name: `fold_bins`: in each device's 1024 traces no bin appears more than 3 times, and some bin appears exactly 3 times.
All inputs are finite; a program needn't handle non-finite values.
Results may differ from the reference program's by a relative error of at most 0.0003.
Values may be sent and summed in bfloat16 or wider, within the bound.
A program may use at most 192 MiB of HBM per device.

```python
import jax
import jax.numpy as jnp
from jax import lax

NT = 1536
LAGR = 20
TBLK = 128
RT_MAX = 8
RS = 2
MOST = 3
IL_DEV = 2
BINS_PER_TILE = 1024
TR_DEV = 1024
TRACES = 262144
IL = 8
XL = 512
N_SHOT = 64
N_INLINE = 4


def draw_radii(key, part):
    key_vals, key_pos = jax.random.split(jax.random.fold_in(key, 17))
    blocks = NT // TBLK
    chosen = jax.random.randint(key_vals, (blocks,), 1, RT_MAX + 1)
    position = jax.random.randint(key_pos, (), 0, blocks)
    places = jnp.arange(blocks)
    chosen = jnp.where(places == (position + 1) % blocks, 1, chosen)
    chosen = jnp.where(places == position, RT_MAX, chosen)
    return chosen.astype(jnp.int32)


def draw_fold_bins(key, part):
    base = jax.random.fold_in(key, 29)
    device_total = TRACES // TR_DEV
    bin_index = jnp.arange(BINS_PER_TILE, dtype=jnp.int32)
    slot = jnp.arange(TR_DEV, dtype=jnp.int32)

    def one_device(device):
        tile = device % N_INLINE
        inline_tile_position = jax.random.permutation(jax.random.fold_in(base, 100000 + tile), BINS_PER_TILE).astype(jnp.int32)
        key_noise, key_heavy, key_shuffle = jax.random.split(jax.random.fold_in(base, device), 3)
        random_jitter = jax.random.randint(key_noise, (BINS_PER_TILE,), 0, 1 << 20).astype(jnp.int32)
        extra_reward = jnp.where(inline_tile_position < 4 + BINS_PER_TILE // 8, 1 << 19, 0).astype(jnp.int32)
        ordering_rank = jnp.where(inline_tile_position < 4, 0, random_jitter + extra_reward + 1).astype(jnp.int32)
        score = ordering_rank * BINS_PER_TILE + bin_index
        order = jnp.argsort(-score).astype(jnp.int32)
        heavy = jax.random.randint(key_heavy, (), BINS_PER_TILE // 16, BINS_PER_TILE // 8 + 1).astype(jnp.int32)
        rank = jnp.where(slot < MOST * heavy, slot // MOST, heavy + slot - MOST * heavy)
        chosen = order[rank]
        return chosen[jax.random.permutation(key_shuffle, TR_DEV)]
    every = jax.vmap(one_device)(jnp.arange(device_total, dtype=jnp.int32))
    return every.reshape(TRACES, 1).astype(jnp.int32)


def level_of(rng, shape, shards, least, high):
    factor_of = 1.0
    for axis_at, blocks in shards:
        steps = jax.random.uniform(jax.random.fold_in(jax.random.fold_in(rng, 6), axis_at), (blocks,), jnp.float32, least / len(shards), high / len(shards))
        factor_of = factor_of * jnp.repeat(jnp.exp(steps), shape[axis_at] // blocks).reshape((-1,) + (1,) * (len(shape) - 1 - axis_at))
    return factor_of


def noise(own_key, shape, deviation, most, pieces=(), kind=jnp.bfloat16):
    level = level_of(own_key, shape, pieces, -0.22, 0.18) if pieces else 1.0
    values = jax.random.normal(own_key, shape, jnp.float32) * deviation * level
    return jnp.minimum(jnp.maximum(values, -most), most).astype(kind)


def setup_inputs(seed: int = 0) -> dict:
    key_list = jax.random.split(jax.random.key(seed), 4)
    return {
        "traces": noise(key_list[0], (TRACES, 2, NT), 1.0, 6.0, ((0, 256),)),
        "fold_bins": draw_fold_bins(jax.random.fold_in(key_list[3], 71), 0),
        "radii": draw_radii(jax.random.fold_in(key_list[3], 71), 0),
    }


EPS = 1e-06

def time_weights(radii):
    radius_t = jnp.repeat(radii, TBLK).astype(jnp.float32)
    offsets = jnp.abs(jnp.arange(-RT_MAX, RT_MAX + 1)).astype(jnp.float32)
    return jnp.maximum(radius_t[None, :] + 1.0 - offsets[:, None], 0.0) / ((radius_t + 1.0) ** 2)[None, :]

def temporal_smoother(values, weights):
    padded = jnp.pad(values, [(0, 0)] * (values.ndim - 1) + [(RT_MAX, RT_MAX)])
    summed = weights[0] * padded[..., 0:NT]
    for offset in range(1, 2 * RT_MAX + 1):
        summed = summed + weights[offset] * padded[..., offset:offset + NT]
    return summed

def space_smooth(values, along):
    span_len = values.shape[along] - 2 * RS
    summed = None
    for offset in range(2 * RS + 1):
        weight = (RS + 1 - abs(offset - RS)) / float((RS + 1) ** 2)
        piece = weight * lax.slice_in_dim(values, offset, offset + span_len, axis=along)
        summed = piece if summed is None else summed + piece
    return summed

def spatial(values):
    padded = jnp.pad(values, [(RS, RS), (RS, RS)] + [(0, 0)] * (values.ndim - 2))
    return space_smooth(space_smooth(padded, 0), 1)

def reference(traces, fold_bins, radii):
    device_count = N_SHOT * N_INLINE
    trace_rows = traces.reshape(device_count, TR_DEV, 2 * NT)
    bin_ids = fold_bins.reshape(device_count, TR_DEV)

    def add_block(carry, block_items):
        sums, counts = carry
        block_rows, block_bins, device = block_items
        tile_index = device % N_INLINE
        segment = (tile_index * IL_DEV + block_bins % IL_DEV) * XL + block_bins // IL_DEV
        sums = sums + jax.ops.segment_sum(block_rows.astype(jnp.float32), segment, num_segments=IL * XL)
        counts = counts + jax.ops.segment_sum(jnp.ones((TR_DEV,), jnp.float32), segment, num_segments=IL * XL)
        return ((sums, counts), None)
    start = (jnp.zeros((IL * XL, 2 * NT), jnp.float32), jnp.zeros((IL * XL,), jnp.float32))
    (sums, counts), _ = lax.scan(add_block, start, (trace_rows, bin_ids, jnp.arange(device_count, dtype=jnp.int32)))
    stacks = (sums / jnp.maximum(counts, 1.0)[:, None]).reshape(IL, XL, 2, NT)
    baseline = stacks[:, :, 0]
    monitor = stacks[:, :, 1]
    weights = time_weights(radii)
    benergy = spatial(temporal_smoother(baseline * baseline, weights))
    monitor_padded_volume = jnp.pad(monitor, ((0, 0), (0, 0), (LAGR, LAGR)))

    def one_lag(lag_index):
        shifted = lax.dynamic_slice_in_dim(monitor_padded_volume, (lag_index + LAGR).astype(jnp.int32), NT, axis=2)
        cross_term = spatial(temporal_smoother(baseline * shifted, weights))
        menergy = spatial(temporal_smoother(shifted * shifted, weights))
        return cross_term / jnp.sqrt((benergy + EPS) * (menergy + EPS))
    similarity = lax.map(one_lag, jnp.arange(-LAGR, LAGR + 1, dtype=jnp.int32))
    return jnp.transpose(similarity, (1, 2, 0, 3))
```

```python
import jax
import jax.numpy as jnp
from jax import lax
from jax.experimental import pallas as pl
from jax.experimental.pallas import tpu as pltpu
from jax.sharding import PartitionSpec as P

NT = 1536
LAGR = 20
NLAG = 2 * LAGR + 1
TBLK = 128
NBLK = NT // TBLK
RT_MAX = 8
RS = 2
IL_DEV = 2
XL_DEV = 8
EPS = 1e-06

IL_H = IL_DEV + 2 * RS
XL_H = XL_DEV + 2 * RS
BINS = IL_DEV * XL_DEV
BINS_H = IL_H * XL_H
OCT = 6
LANES = 128
EDGE = LANES + LANES // 2
WIDE = NT + 2 * EDGE
BAND = 288


def band_matrices(radii):
    row = jnp.arange(2)[:, None] * 8 + jnp.arange(BAND)[None, :] - 84
    offset = jnp.abs(row[None, :, :, None] - jnp.arange(TBLK)[None, None, None, :])
    weight = jnp.maximum(radii[:, None, None, None] + 1 - offset, 0)
    sample = jnp.arange(NBLK)[:, None, None] * TBLK + row[None]
    inside = (sample >= 0) & (sample < NT)
    return jnp.where(inside[..., None], weight, 0).astype(jnp.bfloat16)


def triangle(cells):
    count = len(cells)
    pair = [cells[i] + cells[i + 1] for i in range(count - 1)]
    box = [pair[i] + cells[i + 2] for i in range(count - 2)]
    pair = [box[i] + box[i + 1] for i in range(count - 3)]
    return [pair[i] + box[i + 2] for i in range(count - 4)]


def space_smooth(cell):
    columns = [triangle([cell(il, xl) for il in range(IL_H)]) for xl in range(XL_H)]
    return [triangle([columns[xl][il] for xl in range(XL_H)]) for il in range(IL_DEV)]


def split_store(ref, rows, value):
    high = value.astype(jnp.bfloat16)
    ref[0, rows, LANES:] = high
    ref[1, rows, LANES:] = (value - high.astype(jnp.float32)).astype(jnp.bfloat16)


def similarity_kernel(eps_ref, bm_ref, band_ref, out_ref, base, turned, lagged, smooth, bsmooth, bline, bscale):
    step = pl.program_id(0)

    def tile(which, index):
        return bm_ref[which, :, pl.ds(pl.multiple_of((step + index) * LANES, LANES), LANES)]

    lane = lax.broadcasted_iota(jnp.int32, (8, LANES), 1)
    sub = lax.broadcasted_iota(jnp.int32, (8, LANES), 0)
    source = (lane + sub) % LANES
    stays = lane + sub < LANES

    def turn(row):
        return jnp.take_along_axis(jnp.broadcast_to(row, (8, LANES)), source, axis=1)

    @pl.when(step == 0)
    def _():
        for row in range(BINS_H):
            turned[row] = turn(bm_ref[1, row:row + 1, LANES:2 * LANES])

    later = tile(1, 2)
    for row in range(BINS_H):
        fresh = turn(later[row:row + 1, :])
        lagged[row] = jnp.where(stays, turned[row], fresh)
        turned[row] = fresh

    lanes = lax.broadcasted_iota(jnp.int32, (BINS_H, LANES), 1)
    for octet in range(OCT):
        shift = 8 * octet - LAGR
        if shift > 0:
            mixed = jnp.where(lanes < LANES - shift, tile(0, 1), tile(0, 0))
        else:
            mixed = jnp.where(lanes >= -shift, tile(0, 1), tile(0, 2))
        base[octet] = pltpu.roll(mixed, shift % LANES, axis=1)

    smooth[:, :, :LANES] = smooth[:, :, LANES:]
    bsmooth[:, :, :LANES] = bsmooth[:, :, LANES:]
    for octet in range(OCT + 1):
        def cell(il, xl):
            row = il * XL_H + xl
            moved = lagged[row]
            if octet == OCT:
                return moved * moved
            return base[octet, row:row + 1, :] * moved
        for il, cells in enumerate(space_smooth(cell)):
            for xl in range(0, XL_DEV, 2):
                first = octet * 8 * BINS + (il * XL_DEV + xl) * 8
                split_store(smooth, slice(first, first + 16), jnp.concatenate([cells[xl], cells[xl + 1]], axis=0))

    energy = [base[3, il * XL_H:(il + 1) * XL_H, :] for il in range(IL_H)]
    energy = triangle([value * value for value in energy])
    for il in range(IL_DEV):
        bline[il, :XL_H, :] = energy[il]
    parts = [triangle([bline[il, k:k + XL_DEV, :] for k in range(2 * RS + 1)])[0] for il in range(IL_DEV)]
    split_store(bsmooth, slice(0, BINS), jnp.concatenate(parts, axis=0))

    @pl.when(step > 0)
    def _():
        eps = eps_ref[jnp.maximum(step - 1, 0)]

        def smoothed(ref, rows, band):
            return jnp.dot(ref[0, rows, :], band, preferred_element_type=jnp.float32) + jnp.dot(
                ref[1, rows, :], band, preferred_element_type=jnp.float32
            )

        def band_of(octet):
            start = 40 - 8 * octet
            return band_ref[0, (start // 8) % 2, start // 16 * 16:start // 16 * 16 + 2 * LANES, :]

        bscale[...] = lax.rsqrt(smoothed(bsmooth, slice(0, BINS), band_of(3)) + eps)
        for octet in range(OCT):
            band = band_of(octet)
            cross = smoothed(smooth, slice(octet * 8 * BINS, (octet + 1) * 8 * BINS), band)
            menergy = smoothed(smooth, slice(OCT * 8 * BINS, (OCT + 1) * 8 * BINS), band)
            value = cross * lax.rsqrt(menergy + eps)
            value = value.reshape(IL_DEV, XL_DEV, 8, LANES)
            value = value * bscale[...].reshape(IL_DEV, XL_DEV, 1, LANES)
            count = min(8, NLAG - 8 * octet)
            out_ref[:, :, 8 * octet:8 * octet + count, :] = value[:, :, :count, :]


def similarity(bm, radii):
    eps = EPS * 81.0 * (radii.astype(jnp.float32) + 1.0) ** 2
    return pl.pallas_call(
        similarity_kernel,
        grid=(NBLK + 1,),
        out_shape=jax.ShapeDtypeStruct((IL_DEV, XL_DEV, NLAG, NT), jnp.float32),
        in_specs=[
            pl.BlockSpec(memory_space=pltpu.SMEM),
            pl.BlockSpec((2, BINS_H, WIDE), lambda j: (0, 0, 0)),
            pl.BlockSpec((1, 2, BAND, TBLK), lambda j: (jnp.maximum(j - 1, 0), 0, 0, 0)),
        ],
        out_specs=pl.BlockSpec((IL_DEV, XL_DEV, NLAG, TBLK), lambda j: (0, 0, 0, jnp.maximum(j - 1, 0))),
        scratch_shapes=[
            pltpu.VMEM((OCT, BINS_H, LANES), jnp.float32),
            pltpu.VMEM((BINS_H, 8, LANES), jnp.float32),
            pltpu.VMEM((BINS_H, 8, LANES), jnp.float32),
            pltpu.VMEM((2, (OCT + 1) * 8 * BINS, 2 * LANES), jnp.bfloat16),
            pltpu.VMEM((2, BINS, 2 * LANES), jnp.bfloat16),
            pltpu.VMEM((IL_DEV, 16, LANES), jnp.float32),
            pltpu.VMEM((BINS, LANES), jnp.float32),
        ],
        compiler_params=pltpu.CompilerParams(vmem_limit_bytes=48 << 20),
        name="similarity",
    )(eps, bm, band_matrices(radii))


def with_halo(cells, sides, width):
    for axis, dim in sides:
        count = lax.axis_size(axis)
        ends = count - 1
        head = lax.slice_in_dim(cells, 0, width, axis=dim)
        tail = lax.slice_in_dim(cells, cells.shape[dim] - width, cells.shape[dim], axis=dim)
        cells = jnp.concatenate(
            [
                lax.ppermute(tail, axis, [(i, (i + 1) % count) for i in range(ends)]),
                cells,
                lax.ppermute(head, axis, [((i + 1) % count, i) for i in range(ends)]),
            ],
            axis=dim,
        )
    return cells


def shards(traces, fold_bins, radii):
    n_shot = lax.axis_size("shot")
    bins_dev = IL_DEV * XL_DEV
    bins_tile = bins_dev * n_shot
    trace_count = traces.shape[0]
    trace_rows = traces.reshape(trace_count, 2 * NT)
    bin_ids = fold_bins[:, 0]
    onehot = (bin_ids[:, None] == jnp.arange(bins_tile, dtype=jnp.int32)[None, :]).astype(jnp.int32)
    counts_local = jnp.sum(onehot, axis=0)
    partial_sums = jnp.dot(
        onehot.T.astype(jnp.bfloat16), trace_rows, preferred_element_type=jnp.float32
    )
    stacked_sums, fold_count = (
        lax.psum_scatter(partial_sums, "shot", scatter_dimension=0, tiled=True),
        lax.psum_scatter(counts_local.astype(jnp.float32), "shot", scatter_dimension=0, tiled=True),
    )
    stacks = stacked_sums / jnp.maximum(fold_count, 1.0)[:, None]
    stack_grid = jnp.transpose(stacks.reshape(XL_DEV, IL_DEV, 2, NT), (1, 0, 2, 3))
    haloed = with_halo(stack_grid, (("inline", 0), ("shot", 1)), RS)
    bm = jnp.transpose(haloed.reshape(BINS_H, 2, NT), (1, 0, 2))
    bm = jnp.pad(bm, ((0, 0), (0, 0), (EDGE, EDGE)))
    return similarity(bm, radii)


def solution(mesh):
    placed = (P(("shot", "inline"), None, None), P(("shot", "inline"), None), P())
    return jax.shard_map(
        shards,
        mesh=mesh,
        in_specs=placed,
        out_specs=P("inline", "shot", None, None),
        check_vma=False,
    )
```

```python
import functools

import jax
import jax.numpy as jnp
from jax import lax
from jax.experimental import pallas as pl
from jax.experimental.pallas import tpu as pltpu
from jax.sharding import PartitionSpec as P

NT = 1536
LAGR = 20
NLAG = 2 * LAGR + 1
TBLK = 128
NBLK = NT // TBLK
RT_MAX = 8
RS = 2
IL_DEV = 2
XL_DEV = 8
EPS = 1e-06

IL_H = IL_DEV + 2 * RS
XL_H = XL_DEV + 2 * RS
BINS = IL_DEV * XL_DEV
BINS_H = IL_H * XL_H
OCT = 6
LANES = 128
EDGE = LANES + LANES // 2
WIDE = NT + 2 * EDGE
BAND = 288


def band_matrices(radii):
    row = jnp.arange(2)[:, None] * 8 + jnp.arange(BAND)[None, :] - 84
    offset = jnp.abs(row[None, :, :, None] - jnp.arange(TBLK)[None, None, None, :])
    weight = jnp.maximum(radii[:, None, None, None] + 1 - offset, 0)
    sample = jnp.arange(NBLK)[:, None, None] * TBLK + row[None]
    inside = (sample >= 0) & (sample < NT)
    return jnp.where(inside[..., None], weight, 0).astype(jnp.bfloat16)


def triangle(cells):
    count = len(cells)
    pair = [cells[i] + cells[i + 1] for i in range(count - 1)]
    box = [pair[i] + cells[i + 2] for i in range(count - 2)]
    pair = [box[i] + box[i + 1] for i in range(count - 3)]
    return [pair[i] + box[i + 2] for i in range(count - 4)]


def space_smooth(cell):
    columns = [triangle([cell(il, xl) for il in range(IL_H)]) for xl in range(XL_H)]
    return [triangle([columns[xl][il] for xl in range(XL_H)]) for il in range(IL_DEV)]


def split_store(ref, rows, value):
    high = value.astype(jnp.bfloat16)
    ref[0, rows, LANES:] = high
    ref[1, rows, LANES:] = (value - high.astype(jnp.float32)).astype(jnp.bfloat16)


def similarity_kernel(eps_ref, bm_ref, band_ref, out_ref, base, turned, lagged, smooth, bsmooth, bline, bscale):
    step = pl.program_id(0)

    def tile(which, index):
        return bm_ref[which, :, pl.ds(pl.multiple_of((step + index) * LANES, LANES), LANES)]

    lane = lax.broadcasted_iota(jnp.int32, (8, LANES), 1)
    sub = lax.broadcasted_iota(jnp.int32, (8, LANES), 0)
    source = (lane + sub) % LANES
    stays = lane + sub < LANES

    def turn(row):
        return jnp.take_along_axis(jnp.broadcast_to(row, (8, LANES)), source, axis=1)

    @pl.when(step == 0)
    def _():
        for row in range(BINS_H):
            turned[row] = turn(bm_ref[1, row:row + 1, LANES:2 * LANES])

    later = tile(1, 2)
    for row in range(BINS_H):
        fresh = turn(later[row:row + 1, :])
        lagged[row] = jnp.where(stays, turned[row], fresh)
        turned[row] = fresh

    lanes = lax.broadcasted_iota(jnp.int32, (BINS_H, LANES), 1)
    for octet in range(OCT):
        shift = 8 * octet - LAGR
        if shift > 0:
            mixed = jnp.where(lanes < LANES - shift, tile(0, 1), tile(0, 0))
        else:
            mixed = jnp.where(lanes >= -shift, tile(0, 1), tile(0, 2))
        base[octet] = pltpu.roll(mixed, shift % LANES, axis=1)

    smooth[:, :, :LANES] = smooth[:, :, LANES:]
    bsmooth[:, :, :LANES] = bsmooth[:, :, LANES:]
    for octet in range(OCT + 1):
        def cell(il, xl):
            row = il * XL_H + xl
            moved = lagged[row]
            if octet == OCT:
                return moved * moved
            return base[octet, row:row + 1, :] * moved
        for il, cells in enumerate(space_smooth(cell)):
            for xl in range(0, XL_DEV, 2):
                first = octet * 8 * BINS + (il * XL_DEV + xl) * 8
                split_store(smooth, slice(first, first + 16), jnp.concatenate([cells[xl], cells[xl + 1]], axis=0))

    energy = [base[3, il * XL_H:(il + 1) * XL_H, :] for il in range(IL_H)]
    energy = triangle([value * value for value in energy])
    for il in range(IL_DEV):
        bline[il, :XL_H, :] = energy[il]
    parts = [triangle([bline[il, k:k + XL_DEV, :] for k in range(2 * RS + 1)])[0] for il in range(IL_DEV)]
    split_store(bsmooth, slice(0, BINS), jnp.concatenate(parts, axis=0))

    @pl.when(step > 0)
    def _():
        eps = eps_ref[jnp.maximum(step - 1, 0)]

        def smoothed(ref, rows, band):
            return jnp.dot(ref[0, rows, :], band, preferred_element_type=jnp.float32) + jnp.dot(
                ref[1, rows, :], band, preferred_element_type=jnp.float32
            )

        def band_of(octet):
            start = 40 - 8 * octet
            return band_ref[0, (start // 8) % 2, start // 16 * 16:start // 16 * 16 + 2 * LANES, :]

        bscale[...] = lax.rsqrt(smoothed(bsmooth, slice(0, BINS), band_of(3)) + eps)
        for octet in range(OCT):
            band = band_of(octet)
            cross = smoothed(smooth, slice(octet * 8 * BINS, (octet + 1) * 8 * BINS), band)
            menergy = smoothed(smooth, slice(OCT * 8 * BINS, (OCT + 1) * 8 * BINS), band)
            value = cross * lax.rsqrt(menergy + eps)
            value = value.reshape(IL_DEV, XL_DEV, 8, LANES)
            value = value * bscale[...].reshape(IL_DEV, XL_DEV, 1, LANES)
            count = min(8, NLAG - 8 * octet)
            out_ref[:, :, 8 * octet:8 * octet + count, :] = value[:, :, :count, :]


def similarity(bm, radii):
    eps = EPS * 81.0 * (radii.astype(jnp.float32) + 1.0) ** 2
    return pl.pallas_call(
        similarity_kernel,
        grid=(NBLK + 1,),
        out_shape=jax.ShapeDtypeStruct((IL_DEV, XL_DEV, NLAG, NT), jnp.float32),
        in_specs=[
            pl.BlockSpec(memory_space=pltpu.SMEM),
            pl.BlockSpec((2, BINS_H, WIDE), lambda j: (0, 0, 0)),
            pl.BlockSpec((1, 2, BAND, TBLK), lambda j: (jnp.maximum(j - 1, 0), 0, 0, 0)),
        ],
        out_specs=pl.BlockSpec((IL_DEV, XL_DEV, NLAG, TBLK), lambda j: (0, 0, 0, jnp.maximum(j - 1, 0))),
        scratch_shapes=[
            pltpu.VMEM((OCT, BINS_H, LANES), jnp.float32),
            pltpu.VMEM((BINS_H, 8, LANES), jnp.float32),
            pltpu.VMEM((BINS_H, 8, LANES), jnp.float32),
            pltpu.VMEM((2, (OCT + 1) * 8 * BINS, 2 * LANES), jnp.bfloat16),
            pltpu.VMEM((2, BINS, 2 * LANES), jnp.bfloat16),
            pltpu.VMEM((IL_DEV, 16, LANES), jnp.float32),
            pltpu.VMEM((BINS, LANES), jnp.float32),
        ],
        compiler_params=pltpu.CompilerParams(vmem_limit_bytes=48 << 20),
        name="similarity",
    )(eps, bm, band_matrices(radii))


MESH = pl.DeviceIdType.MESH
RING_X = 4
CHUNK = 2 * LANES
X_FIRST = (0, 1, 3, 5, 6, 8, 10)
PACE = 2


def chunk_order(chunks, last):
    pairs = [(chunk + PACE * op, op, chunk) for chunk in range(chunks) for op in range(last + 1)]
    return [(chunk, op) for _, op, chunk in sorted(pairs)]


def stack_kernel(sizes, ids_ref, rows_ref, out_ref, peer_ids, peer, hot, hot_peer, part, count, count_in, x_big, z_big,
                 x_small, z_small, y_in, s_in, s_out, own, fold, pair_sem, ring_sem, count_sem, y_sem, s_sem):
    chunks, nx, nz, ny = sizes
    shot = lax.axis_index("shot")
    line = lax.axis_index("inline")
    n_shot = 2 * nx * nz
    core = shot % 2
    mx = shot // (2 * nz)
    mz = (shot // 2) % nz
    extent = {"x": nx, "z": nz}
    place = {"x": mx, "z": mz}

    def along(axis, by):
        if axis == "x":
            return ((mx + by + nx) % nx) * (2 * nz) + mz * 2 + core
        return mx * (2 * nz) + ((mz + by + nz) % nz) * 2 + core

    pair = shot + 1 - 2 * core
    partners = [(pair, line)]
    partners += [(along(axis, by), line) for axis in "xz" for by in (1, -1)]
    partners += [(shot, (line + 1) % ny), (shot, (line + ny - 1) % ny)]
    partners += [((shot + 1) % n_shot, line), ((shot + n_shot - 1) % n_shot, line)]
    barrier = pltpu.get_barrier_semaphore()
    for partner in partners:
        pl.semaphore_signal(barrier, inc=1, device_id=partner, device_id_type=MESH)
    pl.semaphore_wait(barrier, len(partners))

    sent = []

    def send(source, target, sems, index, device, when=None):
        copy = pltpu.make_async_remote_copy(
            src_ref=source, dst_ref=target, send_sem=sems.at[(0, *index)], recv_sem=sems.at[(1, *index)],
            device_id=device, device_id_type=MESH,
        )
        if when is None:
            copy.start()
        else:
            pl.when(when)(copy.start)
        sent.append((copy, when))
        return copy

    def arrive(buffer, sems, index, when=None):
        copy = pltpu.make_async_remote_copy(
            src_ref=buffer, dst_ref=buffer, send_sem=sems.at[(0, *index)], recv_sem=sems.at[(1, *index)],
            device_id=(pair, line), device_id_type=MESH,
        )
        if when is None:
            copy.wait_recv()
        else:
            pl.when(when)(copy.wait_recv)

    send(ids_ref, peer_ids, pair_sem, (chunks,), (pair, line))
    for chunk in range(chunks):
        send(rows_ref.at[chunk], peer.at[chunk], pair_sem, (chunk,), (pair, line))

    @pl.when(line == 0)
    def _():
        y_in[0] = jnp.zeros_like(y_in[0])

    @pl.when(line == ny - 1)
    def _():
        y_in[1] = jnp.zeros_like(y_in[1])

    @pl.when(shot == 0)
    def _():
        s_in[0] = jnp.zeros_like(s_in[0])

    @pl.when(shot == n_shot - 1)
    def _():
        s_in[1] = jnp.zeros_like(s_in[1])

    out_ref[...] = jnp.zeros_like(out_ref)

    bins = nx * nz * BINS

    def one_hot(ids, target):
        def block(i, carry):
            row = lax.broadcasted_iota(jnp.int32, (32, 1), 0) + i * 32
            cell = row % BINS
            name = (row // BINS) * (2 * BINS) + core * BINS + (cell % XL_DEV) * IL_DEV + cell // XL_DEV
            target[pl.ds(pl.multiple_of(i * 32, 32), 32), :] = jnp.where(ids == name, 1.0, 0.0).astype(jnp.bfloat16)
            return carry
        lax.fori_loop(0, bins // 32, block, 0)

    one_hot(ids_ref[...], hot)
    arrive(peer_ids, pair_sem, (chunks,))
    one_hot(peer_ids[...], hot_peer)

    contract = (((1,), (1,)), ((), ()))
    ones = jnp.ones((8, hot.shape[1]), jnp.bfloat16)
    wide = nz * BINS
    sub = lax.broadcasted_iota(jnp.int32, (8, wide), 0)
    tile = jnp.zeros((8, wide), jnp.float32)
    for x in range(nx):
        counted = sum(
            lax.dot_general(ones, ref[x * wide:(x + 1) * wide, :], contract, preferred_element_type=jnp.float32)
            for ref in (hot, hot_peer)
        )
        tile = jnp.where(sub == x, counted, tile)
    count[0] = tile

    def ring(axis, sems, index, local, inbox, step, turn):
        n = extent[axis]
        hops = (n // 2, n - 1 - n // 2)
        for way in range(2):
            if step > 0 and step <= hops[way]:
                arrive(inbox(way, step - 1), sems, (*index, way, step - 1))
            if step < hops[way]:
                toward = turn if way == 0 else -turn
                dest = (place[axis] + toward * (hops[way] - step) + n) % n
                source = local(dest)
                if step > 0:
                    held = inbox(way, step - 1)
                    held[...] = held[...] + source[...]
                    source = held
                send(source, inbox(way, step), sems, (*index, way, step), (along(axis, toward), line))

    def settled(axis, inbox):
        n = extent[axis]
        return sum(inbox(way, hop - 1)[...] for way, hop in enumerate((n // 2, n - 1 - n // 2)) if hop > 0)

    first_x = [chunk for chunk in range(chunks) if chunk in X_FIRST]
    first_z = [chunk for chunk in range(chunks) if chunk not in X_FIRST]
    steps_x, steps_z = nx // 2, nz // 2

    def count_op(op):
        if op <= steps_z:
            inbox = lambda way, step: count_in.at[0, way, step]
            ring("z", count_sem, (0,), lambda dest: count.at[0], inbox, op, 1)
            if op == steps_z:
                count[1] = count[0] + settled("z", inbox)
        if op >= steps_z:
            inbox = lambda way, step: count_in.at[1, way, step]
            ring("x", count_sem, (1,), lambda dest: count.at[1], inbox, op - steps_z, 1)
            if op == steps_z + steps_x:
                total = count[1] + settled("x", inbox)
                mine = jnp.sum(jnp.where(sub == mx, total, 0.0), axis=0, keepdims=True)
                lane = lax.broadcasted_iota(jnp.int32, (BINS, wide), 1)
                cell = lax.broadcasted_iota(jnp.int32, (BINS, wide), 0)
                mine = jnp.where(lane == mz * BINS + cell, jnp.broadcast_to(mine, (BINS, wide)), 0.0)
                mine = jnp.sum(mine, axis=1, keepdims=True)
                fold[...] = jnp.broadcast_to(jnp.maximum(mine, 1.0), fold.shape)

    last = steps_x + steps_z + 2

    def chunk_op(chunk, op):
        x_leads = chunk in X_FIRST
        slot = (first_x if x_leads else first_z).index(chunk)
        turn = 1 if slot % 2 == 0 else -1
        axes = "xz" if x_leads else "zx"
        half = steps_x if x_leads else steps_z
        full = steps_x + steps_z
        big, small = (x_big, z_small) if x_leads else (z_big, x_small)
        big_in = lambda way, step: big.at[slot, way, step]
        small_in = lambda way, step: small.at[slot, way, step]
        mine = part.at[chunk, mx] if x_leads else part.at[chunk, :, mz]
        if op == 0:
            arrive(peer.at[chunk], pair_sem, (chunk,))
            summed = jnp.dot(hot[...], rows_ref[chunk], preferred_element_type=jnp.float32) + jnp.dot(
                hot_peer[...], peer[chunk], preferred_element_type=jnp.float32
            )
            part[chunk] = summed.reshape(nx, nz, BINS, CHUNK)
        if op <= half:
            local = (lambda dest: part.at[chunk, dest]) if x_leads else (lambda dest: part.at[chunk, :, dest])
            ring(axes[0], ring_sem, (chunk, 0), local, big_in, op, turn)
            if op == half:
                mine[...] = mine[...] + settled(axes[0], big_in)
        if half <= op <= full:
            local = (lambda dest: part.at[chunk, mx, dest]) if x_leads else (lambda dest: part.at[chunk, dest, mz])
            ring(axes[1], ring_sem, (chunk, 1), local, small_in, op - half, turn)
            if op == full:
                stacks = (part[chunk, mx, mz] + settled(axes[1], small_in)) / fold[:, :1]
                own[chunk] = stacks
                send(own.at[chunk], y_in.at[0, chunk], y_sem, (0, chunk), (shot, (line + 1) % ny), line < ny - 1)
                send(own.at[chunk], y_in.at[1, chunk], y_sem, (1, chunk), (shot, (line + ny - 1) % ny), line > 0)
        lanes = slice(EDGE + chunk * LANES, EDGE + (chunk + 1) * LANES)
        if op == full + 1:
            arrive(y_in.at[0, chunk], y_sem, (0, chunk), line > 0)
            arrive(y_in.at[1, chunk], y_sem, (1, chunk), line < ny - 1)
            for group, block in enumerate((y_in[0, chunk], own[chunk], y_in[1, chunk])):
                for which in range(2):
                    for il in range(IL_DEV):
                        cells = block[il * XL_DEV:(il + 1) * XL_DEV, which * LANES:(which + 1) * LANES]
                        inline = group * IL_DEV + il
                        out_ref[which, inline * XL_H + RS:inline * XL_H + RS + XL_DEV, lanes] = cells
                        edge = (which * IL_H + inline) * RS
                        s_out[0, chunk, edge:edge + RS, :] = cells[XL_DEV - RS:, :]
                        s_out[1, chunk, edge:edge + RS, :] = cells[:RS, :]
            send(s_out.at[0, chunk], s_in.at[0, chunk], s_sem, (0, chunk), ((shot + 1) % n_shot, line), shot < n_shot - 1)
            send(s_out.at[1, chunk], s_in.at[1, chunk], s_sem, (1, chunk), ((shot + n_shot - 1) % n_shot, line), shot > 0)
        if op == full + 2:
            arrive(s_in.at[0, chunk], s_sem, (0, chunk), shot > 0)
            arrive(s_in.at[1, chunk], s_sem, (1, chunk), shot < n_shot - 1)
            for side in range(2):
                for which in range(2):
                    for inline in range(IL_H):
                        edge = (which * IL_H + inline) * RS
                        row = inline * XL_H + side * (RS + XL_DEV)
                        out_ref[which, row:row + RS, lanes] = s_in[side, chunk, edge:edge + RS, :]

    for chunk, op in chunk_order(chunks, last):
        if chunk == 0 and op <= steps_x + steps_z:
            count_op(op)
        chunk_op(chunk, op)

    for copy, when in sent:
        if when is None:
            copy.wait_send()
        else:
            pl.when(when)(copy.wait_send)


def haloed_stacks(rows, ids, n_shot, ny, nx=RING_X):
    chunks, traces, _ = rows.shape
    nz = n_shot // (2 * nx)
    leads = len([chunk for chunk in range(chunks) if chunk in X_FIRST])
    cells = (BINS, CHUNK)
    scratch = [
        pltpu.VMEM((1, traces), jnp.int32),
        pltpu.VMEM((chunks, traces, CHUNK), jnp.bfloat16),
        pltpu.VMEM((nx * nz * BINS, traces), jnp.bfloat16),
        pltpu.VMEM((nx * nz * BINS, traces), jnp.bfloat16),
        pltpu.VMEM((chunks, nx, nz, *cells), jnp.float32),
        pltpu.VMEM((2, 8, nz * BINS), jnp.float32),
        pltpu.VMEM((2, 2, max(nx, nz) // 2, 8, nz * BINS), jnp.float32),
        pltpu.VMEM((leads, 2, nx // 2, nz, *cells), jnp.float32),
        pltpu.VMEM((chunks - leads, 2, nz // 2, nx, *cells), jnp.float32),
        pltpu.VMEM((chunks - leads, 2, nx // 2, *cells), jnp.float32),
        pltpu.VMEM((leads, 2, nz // 2, *cells), jnp.float32),
        pltpu.VMEM((2, chunks, *cells), jnp.float32),
        pltpu.VMEM((2, chunks, 2 * IL_H * RS, LANES), jnp.float32),
        pltpu.VMEM((2, chunks, 2 * IL_H * RS, LANES), jnp.float32),
        pltpu.VMEM((chunks, *cells), jnp.float32),
        pltpu.VMEM((BINS, LANES), jnp.float32),
        pltpu.SemaphoreType.DMA((2, chunks + 1)),
        pltpu.SemaphoreType.DMA((2, chunks, 2, 2, max(nx, nz) // 2)),
        pltpu.SemaphoreType.DMA((2, 2, 2, max(nx, nz) // 2)),
        pltpu.SemaphoreType.DMA((2, 2, chunks)),
        pltpu.SemaphoreType.DMA((2, 2, chunks)),
    ]
    vmem = pl.BlockSpec(memory_space=pltpu.VMEM)
    return pl.pallas_call(
        functools.partial(stack_kernel, (chunks, nx, nz, ny)),
        out_shape=jax.ShapeDtypeStruct((2, BINS_H, chunks * LANES + 2 * EDGE), jnp.float32),
        in_specs=[vmem, vmem],
        out_specs=vmem,
        scratch_shapes=scratch,
        compiler_params=pltpu.CompilerParams(
            collective_id=0, has_side_effects=True, vmem_limit_bytes=56 << 20
        ),
        name="stack",
    )(ids, rows)


def shards(traces, fold_bins, radii):
    count = traces.shape[0]
    rows = traces.reshape(count, 2, NBLK, LANES).transpose(2, 0, 1, 3).reshape(NBLK, count, CHUNK)
    bm = haloed_stacks(rows, fold_bins.reshape(1, count), lax.axis_size("shot"), lax.axis_size("inline"))
    return similarity(bm, radii)


def solution(mesh):
    placed = (P(("shot", "inline"), None, None), P(("shot", "inline"), None), P())
    return jax.shard_map(
        shards,
        mesh=mesh,
        in_specs=placed,
        out_specs=P("inline", "shot", None, None),
        check_vma=False,
    )
```

```python
import functools

import jax
import jax.numpy as jnp
from jax import lax
from jax.experimental import pallas as pl
from jax.experimental.pallas import tpu as pltpu
from jax.sharding import PartitionSpec as P

NT = 1536
LAGR = 20
NLAG = 2 * LAGR + 1
TBLK = 128
NBLK = NT // TBLK
RT_MAX = 8
RS = 2
IL_DEV = 2
XL_DEV = 8
EPS = 1e-06

IL_H = IL_DEV + 2 * RS
XL_H = XL_DEV + 2 * RS
BINS = IL_DEV * XL_DEV
BINS_H = IL_H * XL_H
OCT = 6
LANES = 128
EDGE = LANES + LANES // 2
WIDE = NT + 2 * EDGE
BAND = 288


def band_matrices(radii):
    row = jnp.arange(2)[:, None] * 8 + jnp.arange(BAND)[None, :] - 84
    offset = jnp.abs(row[None, :, :, None] - jnp.arange(TBLK)[None, None, None, :])
    weight = jnp.maximum(radii[:, None, None, None] + 1 - offset, 0)
    sample = jnp.arange(NBLK)[:, None, None] * TBLK + row[None]
    inside = (sample >= 0) & (sample < NT)
    return jnp.where(inside[..., None], weight, 0).astype(jnp.bfloat16)


def triangle(cells):
    count = len(cells)
    pair = [cells[i] + cells[i + 1] for i in range(count - 1)]
    box = [pair[i] + cells[i + 2] for i in range(count - 2)]
    pair = [box[i] + box[i + 1] for i in range(count - 3)]
    return [pair[i] + box[i + 2] for i in range(count - 4)]


def space_smooth(cell):
    columns = [triangle([cell(il, xl) for il in range(IL_H)]) for xl in range(XL_H)]
    return [triangle([columns[xl][il] for xl in range(XL_H)]) for il in range(IL_DEV)]


def split_store(ref, rows, value):
    high = value.astype(jnp.bfloat16)
    ref[0, rows, LANES:] = high
    ref[1, rows, LANES:] = (value - high.astype(jnp.float32)).astype(jnp.bfloat16)


def similarity_kernel(eps_ref, bm_ref, band_ref, out_ref, base, turned, lagged, smooth, bsmooth, bline, bscale):
    step = pl.program_id(0)

    def tile(which, index):
        return bm_ref[which, :, pl.ds(pl.multiple_of((step + index) * LANES, LANES), LANES)]

    lane = lax.broadcasted_iota(jnp.int32, (8, LANES), 1)
    sub = lax.broadcasted_iota(jnp.int32, (8, LANES), 0)
    source = (lane + sub) % LANES
    stays = lane + sub < LANES

    def turn(row):
        return jnp.take_along_axis(jnp.broadcast_to(row, (8, LANES)), source, axis=1)

    @pl.when(step == 0)
    def _():
        for row in range(BINS_H):
            turned[row] = turn(bm_ref[1, row:row + 1, LANES:2 * LANES])

    later = tile(1, 2)
    for row in range(BINS_H):
        fresh = turn(later[row:row + 1, :])
        lagged[row] = jnp.where(stays, turned[row], fresh)
        turned[row] = fresh

    lanes = lax.broadcasted_iota(jnp.int32, (BINS_H, LANES), 1)
    for octet in range(OCT):
        shift = 8 * octet - LAGR
        if shift > 0:
            mixed = jnp.where(lanes < LANES - shift, tile(0, 1), tile(0, 0))
        else:
            mixed = jnp.where(lanes >= -shift, tile(0, 1), tile(0, 2))
        base[octet] = pltpu.roll(mixed, shift % LANES, axis=1)

    smooth[:, :, :LANES] = smooth[:, :, LANES:]
    bsmooth[:, :, :LANES] = bsmooth[:, :, LANES:]
    for octet in range(OCT + 1):
        def cell(il, xl):
            row = il * XL_H + xl
            moved = lagged[row]
            if octet == OCT:
                return moved * moved
            return base[octet, row:row + 1, :] * moved
        for il, cells in enumerate(space_smooth(cell)):
            for xl in range(0, XL_DEV, 2):
                first = octet * 8 * BINS + (il * XL_DEV + xl) * 8
                split_store(smooth, slice(first, first + 16), jnp.concatenate([cells[xl], cells[xl + 1]], axis=0))

    energy = [base[3, il * XL_H:(il + 1) * XL_H, :] for il in range(IL_H)]
    energy = triangle([value * value for value in energy])
    for il in range(IL_DEV):
        bline[il, :XL_H, :] = energy[il]
    parts = [triangle([bline[il, k:k + XL_DEV, :] for k in range(2 * RS + 1)])[0] for il in range(IL_DEV)]
    split_store(bsmooth, slice(0, BINS), jnp.concatenate(parts, axis=0))

    @pl.when(step > 0)
    def _():
        eps = eps_ref[jnp.maximum(step - 1, 0)]

        def smoothed(ref, rows, band):
            return jnp.dot(ref[0, rows, :], band, preferred_element_type=jnp.float32) + jnp.dot(
                ref[1, rows, :], band, preferred_element_type=jnp.float32
            )

        def band_of(octet):
            start = 40 - 8 * octet
            return band_ref[0, (start // 8) % 2, start // 16 * 16:start // 16 * 16 + 2 * LANES, :]

        bscale[...] = lax.rsqrt(smoothed(bsmooth, slice(0, BINS), band_of(3)) + eps)
        for octet in range(OCT):
            band = band_of(octet)
            cross = smoothed(smooth, slice(octet * 8 * BINS, (octet + 1) * 8 * BINS), band)
            menergy = smoothed(smooth, slice(OCT * 8 * BINS, (OCT + 1) * 8 * BINS), band)
            value = cross * lax.rsqrt(menergy + eps)
            value = value.reshape(BINS, 8, LANES) * bscale[...].reshape(BINS, 1, LANES)
            count = min(8, NLAG - 8 * octet)
            for cell in range(BINS):
                il, xl = cell // XL_DEV, cell % XL_DEV
                if count == 8:
                    out_ref[il, pl.ds(octet * 8 * XL_DEV + xl, 8, stride=XL_DEV), :] = value[cell]
                else:
                    row = octet * 8 * XL_DEV + xl
                    out_ref[il, row:row + 1, :] = value[cell, :count, :]


def similarity(bm, radii):
    eps = EPS * 81.0 * (radii.astype(jnp.float32) + 1.0) ** 2
    out = pl.pallas_call(
        similarity_kernel,
        grid=(NBLK + 1,),
        out_shape=jax.ShapeDtypeStruct((IL_DEV, NLAG * XL_DEV, NT), jnp.float32),
        in_specs=[
            pl.BlockSpec(memory_space=pltpu.SMEM),
            pl.BlockSpec((2, BINS_H, WIDE), lambda j: (0, 0, 0)),
            pl.BlockSpec((1, 2, BAND, TBLK), lambda j: (jnp.maximum(j - 1, 0), 0, 0, 0)),
        ],
        out_specs=pl.BlockSpec((IL_DEV, NLAG * XL_DEV, TBLK), lambda j: (0, 0, jnp.maximum(j - 1, 0))),
        scratch_shapes=[
            pltpu.VMEM((OCT, BINS_H, LANES), jnp.float32),
            pltpu.VMEM((BINS_H, 8, LANES), jnp.float32),
            pltpu.VMEM((BINS_H, 8, LANES), jnp.float32),
            pltpu.VMEM((2, (OCT + 1) * 8 * BINS, 2 * LANES), jnp.bfloat16),
            pltpu.VMEM((2, BINS, 2 * LANES), jnp.bfloat16),
            pltpu.VMEM((IL_DEV, 16, LANES), jnp.float32),
            pltpu.VMEM((BINS, LANES), jnp.float32),
        ],
        compiler_params=pltpu.CompilerParams(vmem_limit_bytes=48 << 20),
        name="similarity",
    )(eps, bm, band_matrices(radii))
    return jnp.transpose(out.reshape(IL_DEV, NLAG, XL_DEV, NT), (0, 2, 1, 3))


MESH = pl.DeviceIdType.MESH
RING_X = 4
CHUNK = 2 * LANES
X_FIRST = (0, 1, 3, 5, 6, 8, 10)
ORDER = (
    0, 2, 3, 1, 4, 2, 7, 5, 9, 4, 0, 11, 8, 9, 6, 3, 7, 11, 0, 9, 1, 10, 5, 4, 7, 11, 0,
    6, 2, 4, 7, 8, 1, 3, 11, 2, 10, 4, 9, 7, 3, 5, 6, 0, 1, 8, 2, 11, 9, 3, 10, 6, 4, 1,
    5, 7, 8, 2, 3, 10, 6, 11, 1, 5, 4, 8, 0, 9, 10, 6, 3, 1, 5, 2, 8, 11, 7, 9, 10, 6, 0,
    4, 5, 1, 8, 11, 3, 10, 7, 9, 6, 0, 2, 1, 8, 4, 5, 10, 3, 11, 0, 9, 2, 8, 6, 7, 5, 10,
)


def stack_kernel(sizes, ids_ref, rows_ref, out_ref, peer_ids, peer, hot, hot_peer, part, count, count_in, x_big, z_big,
                 x_small, z_small, y_in, s_in, s_out, own, fold, rows, row_sem, pair_sem, ring_sem, count_sem, y_sem, s_sem):
    chunks, nx, nz, ny = sizes
    shot = lax.axis_index("shot")
    line = lax.axis_index("inline")
    n_shot = 2 * nx * nz
    core = shot % 2
    mx = shot // (2 * nz)
    mz = (shot // 2) % nz
    extent = {"x": nx, "z": nz}
    place = {"x": mx, "z": mz}

    def along(axis, by):
        if axis == "x":
            return ((mx + by + nx) % nx) * (2 * nz) + mz * 2 + core
        return mx * (2 * nz) + ((mz + by + nz) % nz) * 2 + core

    pair = shot + 1 - 2 * core
    partners = [(pair, line)]
    partners += [(along(axis, by), line) for axis in "xz" for by in (1, -1)]
    partners += [(shot, (line + 1) % ny), (shot, (line + ny - 1) % ny)]
    partners += [((shot + 1) % n_shot, line), ((shot + n_shot - 1) % n_shot, line)]
    barrier = pltpu.get_barrier_semaphore()
    for partner in partners:
        pl.semaphore_signal(barrier, inc=1, device_id=partner, device_id_type=MESH)

    def block_of(ref, chunk):
        return ref.at[:, :, chunk * LANES:(chunk + 1) * LANES]

    loads = []
    for chunk in range(chunks):
        loads.append(pltpu.make_async_copy(block_of(rows_ref, chunk), block_of(rows, chunk), row_sem.at[chunk]))
        loads[-1].start()

    bins = nx * nz * BINS

    def one_hot(ids, target):
        def block(i, carry):
            row = lax.broadcasted_iota(jnp.int32, (32, 1), 0) + i * 32
            cell = row % BINS
            name = (row // BINS) * (2 * BINS) + core * BINS + (cell % XL_DEV) * IL_DEV + cell // XL_DEV
            target[pl.ds(pl.multiple_of(i * 32, 32), 32), :] = jnp.where(ids == name, 1.0, 0.0).astype(jnp.bfloat16)
            return carry
        lax.fori_loop(0, bins // 32, block, 0)

    one_hot(ids_ref[...], hot)
    out_ref[...] = jnp.zeros_like(out_ref)
    pl.semaphore_wait(barrier, len(partners))

    sent = []

    def send(source, target, sems, index, device, when=None):
        copy = pltpu.make_async_remote_copy(
            src_ref=source, dst_ref=target, send_sem=sems.at[(0, *index)], recv_sem=sems.at[(1, *index)],
            device_id=device, device_id_type=MESH,
        )
        if when is None:
            copy.start()
        else:
            pl.when(when)(copy.start)
        sent.append((copy, when))
        return copy

    def arrive(buffer, sems, index, when=None):
        copy = pltpu.make_async_remote_copy(
            src_ref=buffer, dst_ref=buffer, send_sem=sems.at[(0, *index)], recv_sem=sems.at[(1, *index)],
            device_id=(pair, line), device_id_type=MESH,
        )
        if when is None:
            copy.wait_recv()
        else:
            pl.when(when)(copy.wait_recv)

    def terms(ref, chunk):
        block = block_of(ref, chunk)
        return jnp.concatenate([block[0], block[1]], axis=1)

    send(ids_ref, peer_ids, pair_sem, (chunks,), (pair, line))
    for chunk in range(chunks):
        send(block_of(rows_ref, chunk), block_of(peer, chunk), pair_sem, (chunk,), (pair, line))

    @pl.when(line == 0)
    def _():
        y_in[0] = jnp.zeros_like(y_in[0])

    @pl.when(line == ny - 1)
    def _():
        y_in[1] = jnp.zeros_like(y_in[1])

    @pl.when(shot == 0)
    def _():
        s_in[0] = jnp.zeros_like(s_in[0])

    @pl.when(shot == n_shot - 1)
    def _():
        s_in[1] = jnp.zeros_like(s_in[1])

    arrive(peer_ids, pair_sem, (chunks,))
    one_hot(peer_ids[...], hot_peer)

    contract = (((1,), (1,)), ((), ()))
    ones = jnp.ones((8, hot.shape[1]), jnp.bfloat16)
    wide = nz * BINS
    sub = lax.broadcasted_iota(jnp.int32, (8, wide), 0)
    tile = jnp.zeros((8, wide), jnp.float32)
    for x in range(nx):
        counted = sum(
            lax.dot_general(ones, ref[x * wide:(x + 1) * wide, :], contract, preferred_element_type=jnp.float32)
            for ref in (hot, hot_peer)
        )
        tile = jnp.where(sub == x, counted, tile)
    count[0] = tile

    def ring(axis, sems, index, local, inbox, step, turn):
        n = extent[axis]
        hops = (n // 2, n - 1 - n // 2)
        for way in range(2):
            if step > 0 and step <= hops[way]:
                arrive(inbox(way, step - 1), sems, (*index, way, step - 1))
            if step < hops[way]:
                toward = turn if way == 0 else -turn
                dest = (place[axis] + toward * (hops[way] - step) + n) % n
                source = local(dest)
                if step > 0:
                    held = inbox(way, step - 1)
                    held[...] = held[...] + source[...]
                    source = held
                send(source, inbox(way, step), sems, (*index, way, step), (along(axis, toward), line))

    def settled(axis, inbox):
        n = extent[axis]
        return sum(inbox(way, hop - 1)[...] for way, hop in enumerate((n // 2, n - 1 - n // 2)) if hop > 0)

    first_x = [chunk for chunk in range(chunks) if chunk in X_FIRST]
    first_z = [chunk for chunk in range(chunks) if chunk not in X_FIRST]
    steps_x, steps_z = nx // 2, nz // 2

    def count_op(op):
        if op <= steps_z:
            inbox = lambda way, step: count_in.at[0, way, step]
            ring("z", count_sem, (0,), lambda dest: count.at[0], inbox, op, 1)
            if op == steps_z:
                count[1] = count[0] + settled("z", inbox)
        if op >= steps_z:
            inbox = lambda way, step: count_in.at[1, way, step]
            ring("x", count_sem, (1,), lambda dest: count.at[1], inbox, op - steps_z, 1)
            if op == steps_z + steps_x:
                total = count[1] + settled("x", inbox)
                mine = jnp.sum(jnp.where(sub == mx, total, 0.0), axis=0, keepdims=True)
                lane = lax.broadcasted_iota(jnp.int32, (BINS, wide), 1)
                cell = lax.broadcasted_iota(jnp.int32, (BINS, wide), 0)
                mine = jnp.where(lane == mz * BINS + cell, jnp.broadcast_to(mine, (BINS, wide)), 0.0)
                mine = jnp.sum(mine, axis=1, keepdims=True)
                fold[...] = jnp.broadcast_to(jnp.maximum(mine, 1.0), fold.shape)

    last = steps_x + steps_z + 2

    def chunk_op(chunk, op):
        x_leads = chunk in X_FIRST
        slot = (first_x if x_leads else first_z).index(chunk)
        turn = 1 if slot % 2 == 0 else -1
        axes = "xz" if x_leads else "zx"
        half = steps_x if x_leads else steps_z
        full = steps_x + steps_z
        big, small = (x_big, z_small) if x_leads else (z_big, x_small)
        big_in = lambda way, step: big.at[slot, way, step]
        small_in = lambda way, step: small.at[slot, way, step]
        mine = part.at[chunk, mx] if x_leads else part.at[chunk, :, mz]
        if op == 0:
            arrive(block_of(peer, chunk), pair_sem, (chunk,))
            loads[chunk].wait()
            summed = jnp.dot(hot[...], terms(rows, chunk), preferred_element_type=jnp.float32) + jnp.dot(
                hot_peer[...], terms(peer, chunk), preferred_element_type=jnp.float32
            )
            part[chunk] = summed.reshape(nx, nz, BINS, CHUNK)
        if op <= half:
            local = (lambda dest: part.at[chunk, dest]) if x_leads else (lambda dest: part.at[chunk, :, dest])
            ring(axes[0], ring_sem, (chunk, 0), local, big_in, op, turn)
            if op == half:
                mine[...] = mine[...] + settled(axes[0], big_in)
        if half <= op <= full:
            local = (lambda dest: part.at[chunk, mx, dest]) if x_leads else (lambda dest: part.at[chunk, dest, mz])
            ring(axes[1], ring_sem, (chunk, 1), local, small_in, op - half, turn)
            if op == full:
                stacks = (part[chunk, mx, mz] + settled(axes[1], small_in)) / fold[:, :1]
                own[chunk] = stacks
                send(own.at[chunk], y_in.at[0, chunk], y_sem, (0, chunk), (shot, (line + 1) % ny), line < ny - 1)
                send(own.at[chunk], y_in.at[1, chunk], y_sem, (1, chunk), (shot, (line + ny - 1) % ny), line > 0)
        lanes = slice(EDGE + chunk * LANES, EDGE + (chunk + 1) * LANES)
        if op == full + 1:
            arrive(y_in.at[0, chunk], y_sem, (0, chunk), line > 0)
            arrive(y_in.at[1, chunk], y_sem, (1, chunk), line < ny - 1)
            for group, block in enumerate((y_in[0, chunk], own[chunk], y_in[1, chunk])):
                for which in range(2):
                    for il in range(IL_DEV):
                        cells = block[il * XL_DEV:(il + 1) * XL_DEV, which * LANES:(which + 1) * LANES]
                        inline = group * IL_DEV + il
                        out_ref[which, inline * XL_H + RS:inline * XL_H + RS + XL_DEV, lanes] = cells
                        edge = (which * IL_H + inline) * RS
                        s_out[0, chunk, edge:edge + RS, :] = cells[XL_DEV - RS:, :]
                        s_out[1, chunk, edge:edge + RS, :] = cells[:RS, :]
            send(s_out.at[0, chunk], s_in.at[0, chunk], s_sem, (0, chunk), ((shot + 1) % n_shot, line), shot < n_shot - 1)
            send(s_out.at[1, chunk], s_in.at[1, chunk], s_sem, (1, chunk), ((shot + n_shot - 1) % n_shot, line), shot > 0)
        if op == full + 2:
            arrive(s_in.at[0, chunk], s_sem, (0, chunk), shot > 0)
            arrive(s_in.at[1, chunk], s_sem, (1, chunk), shot < n_shot - 1)
            for side in range(2):
                for which in range(2):
                    for inline in range(IL_H):
                        edge = (which * IL_H + inline) * RS
                        row = inline * XL_H + side * (RS + XL_DEV)
                        out_ref[which, row:row + RS, lanes] = s_in[side, chunk, edge:edge + RS, :]

    done = [0] * chunks
    counted = 0
    for chunk in [chunk for chunk in ORDER if chunk < chunks]:
        op = done[chunk]
        done[chunk] += 1
        if op > last:
            continue
        if op == counted and op <= steps_x + steps_z:
            count_op(op)
            counted += 1
        chunk_op(chunk, op)

    for copy, when in sent:
        if when is None:
            copy.wait_send()
        else:
            pl.when(when)(copy.wait_send)


def haloed_stacks(rows, ids, n_shot, ny, nx=RING_X):
    traces, chunks = rows.shape[1], rows.shape[2] // LANES
    nz = n_shot // (2 * nx)
    leads = len([chunk for chunk in range(chunks) if chunk in X_FIRST])
    cells = (BINS, CHUNK)
    scratch = [
        pltpu.VMEM((1, traces), jnp.int32),
        pltpu.VMEM((2, traces, chunks * LANES), jnp.bfloat16),
        pltpu.VMEM((nx * nz * BINS, traces), jnp.bfloat16),
        pltpu.VMEM((nx * nz * BINS, traces), jnp.bfloat16),
        pltpu.VMEM((chunks, nx, nz, *cells), jnp.float32),
        pltpu.VMEM((2, 8, nz * BINS), jnp.float32),
        pltpu.VMEM((2, 2, max(nx, nz) // 2, 8, nz * BINS), jnp.float32),
        pltpu.VMEM((leads, 2, nx // 2, nz, *cells), jnp.float32),
        pltpu.VMEM((chunks - leads, 2, nz // 2, nx, *cells), jnp.float32),
        pltpu.VMEM((chunks - leads, 2, nx // 2, *cells), jnp.float32),
        pltpu.VMEM((leads, 2, nz // 2, *cells), jnp.float32),
        pltpu.VMEM((2, chunks, *cells), jnp.float32),
        pltpu.VMEM((2, chunks, 2 * IL_H * RS, LANES), jnp.float32),
        pltpu.VMEM((2, chunks, 2 * IL_H * RS, LANES), jnp.float32),
        pltpu.VMEM((chunks, *cells), jnp.float32),
        pltpu.VMEM((BINS, LANES), jnp.float32),
        pltpu.VMEM((2, traces, chunks * LANES), jnp.bfloat16),
        pltpu.SemaphoreType.DMA((chunks,)),
        pltpu.SemaphoreType.DMA((2, chunks + 1)),
        pltpu.SemaphoreType.DMA((2, chunks, 2, 2, max(nx, nz) // 2)),
        pltpu.SemaphoreType.DMA((2, 2, 2, max(nx, nz) // 2)),
        pltpu.SemaphoreType.DMA((2, 2, chunks)),
        pltpu.SemaphoreType.DMA((2, 2, chunks)),
    ]
    vmem = pl.BlockSpec(memory_space=pltpu.VMEM)
    return pl.pallas_call(
        functools.partial(stack_kernel, (chunks, nx, nz, ny)),
        out_shape=jax.ShapeDtypeStruct((2, BINS_H, chunks * LANES + 2 * EDGE), jnp.float32),
        in_specs=[vmem, pl.BlockSpec(memory_space=pl.ANY)],
        out_specs=vmem,
        scratch_shapes=scratch,
        compiler_params=pltpu.CompilerParams(
            collective_id=0, has_side_effects=True, vmem_limit_bytes=56 << 20
        ),
        name="stack",
    )(ids, rows)


def shards(traces, fold_bins, radii):
    count = traces.shape[0]
    bm = haloed_stacks(jnp.transpose(traces, (1, 0, 2)), fold_bins.reshape(1, count), lax.axis_size("shot"), lax.axis_size("inline"))
    return similarity(bm, radii)


def solution(mesh):
    placed = (P(("shot", "inline"), None, None), P(("shot", "inline"), None), P())
    return jax.shard_map(
        shards,
        mesh=mesh,
        in_specs=placed,
        out_specs=P("inline", "shot", None, None),
        check_vma=False,
    )
```

```python
import functools

import jax
import jax.numpy as jnp
from jax import lax
from jax.experimental import pallas as pl
from jax.experimental.pallas import tpu as pltpu
from jax.sharding import PartitionSpec as P

NT = 1536
LAGR = 20
NLAG = 2 * LAGR + 1
TBLK = 128
NBLK = NT // TBLK
RT_MAX = 8
RS = 2
IL_DEV = 2
XL_DEV = 8
EPS = 1e-06

IL_H = IL_DEV + 2 * RS
XL_H = XL_DEV + 2 * RS
BINS = IL_DEV * XL_DEV
BINS_H = IL_H * XL_H
OCT = 6
LANES = 128
EDGE = LANES + LANES // 2
WIDE = NT + 2 * EDGE
BAND = 288


def band_matrices(radii):
    row = jnp.arange(2)[:, None] * 8 + jnp.arange(BAND)[None, :] - 84
    offset = jnp.abs(row[None, :, :, None] - jnp.arange(TBLK)[None, None, None, :])
    weight = jnp.maximum(radii[:, None, None, None] + 1 - offset, 0)
    sample = jnp.arange(NBLK)[:, None, None] * TBLK + row[None]
    inside = (sample >= 0) & (sample < NT)
    return jnp.where(inside[..., None], weight, 0).astype(jnp.bfloat16)


def triangle(cells):
    count = len(cells)
    pair = [cells[i] + cells[i + 1] for i in range(count - 1)]
    box = [pair[i] + cells[i + 2] for i in range(count - 2)]
    pair = [box[i] + box[i + 1] for i in range(count - 3)]
    return [pair[i] + box[i + 2] for i in range(count - 4)]


def space_smooth(cell):
    columns = [triangle([cell(il, xl) for il in range(IL_H)]) for xl in range(XL_H)]
    return [triangle([columns[xl][il] for xl in range(XL_H)]) for il in range(IL_DEV)]


def split_store(ref, rows, value):
    high = value.astype(jnp.bfloat16)
    ref[0, rows, LANES:] = high
    ref[1, rows, LANES:] = (value - high.astype(jnp.float32)).astype(jnp.bfloat16)


def similarity_kernel(radii_ref, bm_ref, band_ref, out_ref, base, turned, lagged, smooth, bsmooth, bline, bscale):
    step = pl.program_id(0)

    def tile(which, index):
        return bm_ref[which, :, pl.ds(pl.multiple_of((step + index) * LANES, LANES), LANES)]

    lane = lax.broadcasted_iota(jnp.int32, (8, LANES), 1)
    sub = lax.broadcasted_iota(jnp.int32, (8, LANES), 0)
    source = (lane + sub) % LANES
    stays = lane + sub < LANES

    def turn(row):
        return jnp.take_along_axis(jnp.broadcast_to(row, (8, LANES)), source, axis=1)

    @pl.when(step == 0)
    def _():
        for row in range(BINS_H):
            turned[row] = turn(bm_ref[1, row:row + 1, LANES:2 * LANES])

    later = tile(1, 2)
    for row in range(BINS_H):
        fresh = turn(later[row:row + 1, :])
        lagged[row] = jnp.where(stays, turned[row], fresh)
        turned[row] = fresh

    lanes = lax.broadcasted_iota(jnp.int32, (BINS_H, LANES), 1)
    for octet in range(OCT):
        shift = 8 * octet - LAGR
        if shift > 0:
            mixed = jnp.where(lanes < LANES - shift, tile(0, 1), tile(0, 0))
        else:
            mixed = jnp.where(lanes >= -shift, tile(0, 1), tile(0, 2))
        base[octet] = pltpu.roll(mixed, shift % LANES, axis=1)

    smooth[:, :, :LANES] = smooth[:, :, LANES:]
    bsmooth[:, :, :LANES] = bsmooth[:, :, LANES:]
    for octet in range(OCT + 1):
        def cell(il, xl):
            row = il * XL_H + xl
            moved = lagged[row]
            if octet == OCT:
                return moved * moved
            return base[octet, row:row + 1, :] * moved
        for il, cells in enumerate(space_smooth(cell)):
            for xl in range(0, XL_DEV, 2):
                first = octet * 8 * BINS + (il * XL_DEV + xl) * 8
                split_store(smooth, slice(first, first + 16), jnp.concatenate([cells[xl], cells[xl + 1]], axis=0))

    energy = [base[3, il * XL_H:(il + 1) * XL_H, :] for il in range(IL_H)]
    energy = triangle([value * value for value in energy])
    for il in range(IL_DEV):
        bline[il, :XL_H, :] = energy[il]
    parts = [triangle([bline[il, k:k + XL_DEV, :] for k in range(2 * RS + 1)])[0] for il in range(IL_DEV)]
    split_store(bsmooth, slice(0, BINS), jnp.concatenate(parts, axis=0))

    @pl.when(step > 0)
    def _():
        eps = EPS * 81.0 * (radii_ref[jnp.maximum(step - 1, 0)].astype(jnp.float32) + 1.0) ** 2

        def smoothed(ref, rows, band):
            return jnp.dot(ref[0, rows, :], band, preferred_element_type=jnp.float32) + jnp.dot(
                ref[1, rows, :], band, preferred_element_type=jnp.float32
            )

        def band_of(octet):
            start = 40 - 8 * octet
            return band_ref[0, (start // 8) % 2, start // 16 * 16:start // 16 * 16 + 2 * LANES, :]

        bscale[...] = lax.rsqrt(smoothed(bsmooth, slice(0, BINS), band_of(3)) + eps)
        for octet in range(OCT):
            band = band_of(octet)
            cross = smoothed(smooth, slice(octet * 8 * BINS, (octet + 1) * 8 * BINS), band)
            menergy = smoothed(smooth, slice(OCT * 8 * BINS, (OCT + 1) * 8 * BINS), band)
            value = cross * lax.rsqrt(menergy + eps)
            value = value.reshape(BINS, 8, LANES) * bscale[...].reshape(BINS, 1, LANES)
            count = min(8, NLAG - 8 * octet)
            for cell in range(BINS):
                il, xl = cell // XL_DEV, cell % XL_DEV
                if count == 8:
                    out_ref[il, pl.ds(octet * 8 * XL_DEV + xl, 8, stride=XL_DEV), :] = value[cell]
                else:
                    row = octet * 8 * XL_DEV + xl
                    out_ref[il, row:row + 1, :] = value[cell, :count, :]


def similarity(bm, bands, radii):
    out = pl.pallas_call(
        similarity_kernel,
        grid=(NBLK + 1,),
        out_shape=jax.ShapeDtypeStruct((IL_DEV, NLAG * XL_DEV, NT), jnp.float32),
        in_specs=[
            pl.BlockSpec(memory_space=pltpu.SMEM),
            pl.BlockSpec((2, BINS_H, WIDE), lambda j: (0, 0, 0)),
            pl.BlockSpec((1, 2, BAND, TBLK), lambda j: (jnp.maximum(j - 1, 0), 0, 0, 0)),
        ],
        out_specs=pl.BlockSpec((IL_DEV, NLAG * XL_DEV, TBLK), lambda j: (0, 0, jnp.maximum(j - 1, 0))),
        scratch_shapes=[
            pltpu.VMEM((OCT, BINS_H, LANES), jnp.float32),
            pltpu.VMEM((BINS_H, 8, LANES), jnp.float32),
            pltpu.VMEM((BINS_H, 8, LANES), jnp.float32),
            pltpu.VMEM((2, (OCT + 1) * 8 * BINS, 2 * LANES), jnp.bfloat16),
            pltpu.VMEM((2, BINS, 2 * LANES), jnp.bfloat16),
            pltpu.VMEM((IL_DEV, 16, LANES), jnp.float32),
            pltpu.VMEM((BINS, LANES), jnp.float32),
        ],
        compiler_params=pltpu.CompilerParams(vmem_limit_bytes=24 << 20),
        name="similarity",
    )(radii, bm, bands)
    return jnp.transpose(out.reshape(IL_DEV, NLAG, XL_DEV, NT), (0, 2, 1, 3))


MESH = pl.DeviceIdType.MESH
RING_X = 4
CHUNK = 2 * LANES
X_FIRST = (0, 1, 3, 5, 6, 8, 10)
ORDER = (
    0, 2, 3, 1, 4, 2, 7, 5, 9, 4, 0, 11, 8, 9, 6, 3, 7, 11, 0, 9, 1, 10, 5, 4, 7, 11, 0,
    6, 2, 4, 7, 8, 1, 3, 11, 2, 10, 4, 9, 7, 3, 5, 6, 0, 1, 8, 2, 11, 9, 3, 10, 6, 4, 1,
    5, 7, 8, 2, 3, 10, 6, 11, 1, 5, 4, 8, 0, 9, 10, 6, 3, 1, 5, 2, 8, 11, 7, 9, 10, 6, 0,
    4, 5, 1, 8, 11, 3, 10, 7, 9, 6, 0, 2, 1, 8, 4, 5, 10, 3, 11, 0, 9, 2, 8, 6, 7, 5, 10,
)


def stack_kernel(sizes, ids_ref, rows_ref, out_ref, peer_ids, peer, hot, hot_peer, part, count, count_in, x_big, z_big,
                 x_small, z_small, y_in, s_in, s_out, own, fold, pair_sem, ring_sem, count_sem, y_sem, s_sem):
    chunks, nx, nz, ny = sizes
    shot = lax.axis_index("shot")
    line = lax.axis_index("inline")
    n_shot = 2 * nx * nz
    core = shot % 2
    mx = shot // (2 * nz)
    mz = (shot // 2) % nz
    extent = {"x": nx, "z": nz}
    place = {"x": mx, "z": mz}

    def along(axis, by):
        if axis == "x":
            return ((mx + by + nx) % nx) * (2 * nz) + mz * 2 + core
        return mx * (2 * nz) + ((mz + by + nz) % nz) * 2 + core

    pair = shot + 1 - 2 * core
    partners = [(pair, line)]
    partners += [(along(axis, by), line) for axis in "xz" for by in (1, -1)]
    partners += [(shot, (line + 1) % ny), (shot, (line + ny - 1) % ny)]
    partners += [((shot + 1) % n_shot, line), ((shot + n_shot - 1) % n_shot, line)]
    barrier = pltpu.get_barrier_semaphore()
    for partner in partners:
        pl.semaphore_signal(barrier, inc=1, device_id=partner, device_id_type=MESH)

    def block_of(ref, chunk):
        return ref.at[:, :, chunk * LANES:(chunk + 1) * LANES]

    bins = nx * nz * BINS

    def one_hot(ids, target):
        def block(i, carry):
            row = lax.broadcasted_iota(jnp.int32, (32, 1), 0) + i * 32
            cell = row % BINS
            name = (row // BINS) * (2 * BINS) + core * BINS + (cell % XL_DEV) * IL_DEV + cell // XL_DEV
            target[pl.ds(pl.multiple_of(i * 32, 32), 32), :] = jnp.where(ids == name, 1.0, 0.0).astype(jnp.bfloat16)
            return carry
        lax.fori_loop(0, bins // 32, block, 0)

    one_hot(ids_ref[...], hot)
    out_ref[...] = jnp.zeros_like(out_ref)
    pl.semaphore_wait(barrier, len(partners))

    sent = []

    def send(source, target, sems, index, device, when=None):
        copy = pltpu.make_async_remote_copy(
            src_ref=source, dst_ref=target, send_sem=sems.at[(0, *index)], recv_sem=sems.at[(1, *index)],
            device_id=device, device_id_type=MESH,
        )
        if when is None:
            copy.start()
        else:
            pl.when(when)(copy.start)
        sent.append((copy, when))
        return copy

    def arrive(buffer, sems, index, when=None):
        copy = pltpu.make_async_remote_copy(
            src_ref=buffer, dst_ref=buffer, send_sem=sems.at[(0, *index)], recv_sem=sems.at[(1, *index)],
            device_id=(pair, line), device_id_type=MESH,
        )
        if when is None:
            copy.wait_recv()
        else:
            pl.when(when)(copy.wait_recv)

    def terms(ref, chunk):
        block = block_of(ref, chunk)
        return jnp.concatenate([block[0], block[1]], axis=1)

    send(ids_ref, peer_ids, pair_sem, (chunks,), (pair, line))
    for chunk in range(chunks):
        send(block_of(rows_ref, chunk), block_of(peer, chunk), pair_sem, (chunk,), (pair, line))

    @pl.when(line == 0)
    def _():
        y_in[0] = jnp.zeros_like(y_in[0])

    @pl.when(line == ny - 1)
    def _():
        y_in[1] = jnp.zeros_like(y_in[1])

    @pl.when(shot == 0)
    def _():
        s_in[0] = jnp.zeros_like(s_in[0])

    @pl.when(shot == n_shot - 1)
    def _():
        s_in[1] = jnp.zeros_like(s_in[1])

    arrive(peer_ids, pair_sem, (chunks,))
    one_hot(peer_ids[...], hot_peer)

    contract = (((1,), (1,)), ((), ()))
    ones = jnp.ones((8, hot.shape[1]), jnp.bfloat16)
    wide = nz * BINS
    sub = lax.broadcasted_iota(jnp.int32, (8, wide), 0)
    tile = jnp.zeros((8, wide), jnp.float32)
    for x in range(nx):
        counted = sum(
            lax.dot_general(ones, ref[x * wide:(x + 1) * wide, :], contract, preferred_element_type=jnp.float32)
            for ref in (hot, hot_peer)
        )
        tile = jnp.where(sub == x, counted, tile)
    count[0] = tile

    def ring(axis, sems, index, local, inbox, step, turn):
        n = extent[axis]
        hops = (n // 2, n - 1 - n // 2)
        for way in range(2):
            if step > 0 and step <= hops[way]:
                arrive(inbox(way, step - 1), sems, (*index, way, step - 1))
            if step < hops[way]:
                toward = turn if way == 0 else -turn
                dest = (place[axis] + toward * (hops[way] - step) + n) % n
                source = local(dest)
                if step > 0:
                    held = inbox(way, step - 1)
                    held[...] = held[...] + source[...]
                    source = held
                send(source, inbox(way, step), sems, (*index, way, step), (along(axis, toward), line))

    def settled(axis, inbox):
        n = extent[axis]
        return sum(inbox(way, hop - 1)[...] for way, hop in enumerate((n // 2, n - 1 - n // 2)) if hop > 0)

    first_x = [chunk for chunk in range(chunks) if chunk in X_FIRST]
    first_z = [chunk for chunk in range(chunks) if chunk not in X_FIRST]
    steps_x, steps_z = nx // 2, nz // 2

    def count_op(op):
        if op <= steps_z:
            inbox = lambda way, step: count_in.at[0, way, step]
            ring("z", count_sem, (0,), lambda dest: count.at[0], inbox, op, 1)
            if op == steps_z:
                count[1] = count[0] + settled("z", inbox)
        if op >= steps_z:
            inbox = lambda way, step: count_in.at[1, way, step]
            ring("x", count_sem, (1,), lambda dest: count.at[1], inbox, op - steps_z, 1)
            if op == steps_z + steps_x:
                total = count[1] + settled("x", inbox)
                mine = jnp.sum(jnp.where(sub == mx, total, 0.0), axis=0, keepdims=True)
                lane = lax.broadcasted_iota(jnp.int32, (BINS, wide), 1)
                cell = lax.broadcasted_iota(jnp.int32, (BINS, wide), 0)
                mine = jnp.where(lane == mz * BINS + cell, jnp.broadcast_to(mine, (BINS, wide)), 0.0)
                mine = jnp.sum(mine, axis=1, keepdims=True)
                fold[...] = jnp.broadcast_to(jnp.maximum(mine, 1.0), fold.shape)

    last = steps_x + steps_z + 2

    def chunk_op(chunk, op):
        x_leads = chunk in X_FIRST
        slot = (first_x if x_leads else first_z).index(chunk)
        turn = 1 if slot % 2 == 0 else -1
        axes = "xz" if x_leads else "zx"
        half = steps_x if x_leads else steps_z
        full = steps_x + steps_z
        big, small = (x_big, z_small) if x_leads else (z_big, x_small)
        big_in = lambda way, step: big.at[slot, way, step]
        small_in = lambda way, step: small.at[slot, way, step]
        mine = part.at[chunk, mx] if x_leads else part.at[chunk, :, mz]
        if op == 0:
            arrive(block_of(peer, chunk), pair_sem, (chunk,))
            summed = jnp.dot(hot[...], terms(rows_ref, chunk), preferred_element_type=jnp.float32) + jnp.dot(
                hot_peer[...], terms(peer, chunk), preferred_element_type=jnp.float32
            )
            part[chunk] = summed.reshape(nx, nz, BINS, CHUNK)
        if op <= half:
            local = (lambda dest: part.at[chunk, dest]) if x_leads else (lambda dest: part.at[chunk, :, dest])
            ring(axes[0], ring_sem, (chunk, 0), local, big_in, op, turn)
            if op == half:
                mine[...] = mine[...] + settled(axes[0], big_in)
        if half <= op <= full:
            local = (lambda dest: part.at[chunk, mx, dest]) if x_leads else (lambda dest: part.at[chunk, dest, mz])
            ring(axes[1], ring_sem, (chunk, 1), local, small_in, op - half, turn)
            if op == full:
                stacks = (part[chunk, mx, mz] + settled(axes[1], small_in)) / fold[:, :1]
                own[chunk] = stacks
                send(own.at[chunk], y_in.at[0, chunk], y_sem, (0, chunk), (shot, (line + 1) % ny), line < ny - 1)
                send(own.at[chunk], y_in.at[1, chunk], y_sem, (1, chunk), (shot, (line + ny - 1) % ny), line > 0)
        lanes = slice(EDGE + chunk * LANES, EDGE + (chunk + 1) * LANES)
        if op == full + 1:
            arrive(y_in.at[0, chunk], y_sem, (0, chunk), line > 0)
            arrive(y_in.at[1, chunk], y_sem, (1, chunk), line < ny - 1)
            for group, block in enumerate((y_in[0, chunk], own[chunk], y_in[1, chunk])):
                for which in range(2):
                    for il in range(IL_DEV):
                        cells = block[il * XL_DEV:(il + 1) * XL_DEV, which * LANES:(which + 1) * LANES]
                        inline = group * IL_DEV + il
                        out_ref[which, inline * XL_H + RS:inline * XL_H + RS + XL_DEV, lanes] = cells
                        edge = (which * IL_H + inline) * RS
                        s_out[0, chunk, edge:edge + RS, :] = cells[XL_DEV - RS:, :]
                        s_out[1, chunk, edge:edge + RS, :] = cells[:RS, :]
            send(s_out.at[0, chunk], s_in.at[0, chunk], s_sem, (0, chunk), ((shot + 1) % n_shot, line), shot < n_shot - 1)
            send(s_out.at[1, chunk], s_in.at[1, chunk], s_sem, (1, chunk), ((shot + n_shot - 1) % n_shot, line), shot > 0)
        if op == full + 2:
            arrive(s_in.at[0, chunk], s_sem, (0, chunk), shot > 0)
            arrive(s_in.at[1, chunk], s_sem, (1, chunk), shot < n_shot - 1)
            for side in range(2):
                for which in range(2):
                    for inline in range(IL_H):
                        edge = (which * IL_H + inline) * RS
                        row = inline * XL_H + side * (RS + XL_DEV)
                        out_ref[which, row:row + RS, lanes] = s_in[side, chunk, edge:edge + RS, :]

    done = [0] * chunks
    counted = 0
    for chunk in [chunk for chunk in ORDER if chunk < chunks]:
        op = done[chunk]
        done[chunk] += 1
        if op > last:
            continue
        if op == counted and op <= steps_x + steps_z:
            count_op(op)
            counted += 1
        chunk_op(chunk, op)

    for copy, when in sent:
        if when is None:
            copy.wait_send()
        else:
            pl.when(when)(copy.wait_send)


def haloed_stacks(rows, ids, n_shot, ny, nx=RING_X):
    traces, chunks = rows.shape[1], rows.shape[2] // LANES
    nz = n_shot // (2 * nx)
    leads = len([chunk for chunk in range(chunks) if chunk in X_FIRST])
    cells = (BINS, CHUNK)
    scratch = [
        pltpu.VMEM((1, traces), jnp.int32),
        pltpu.VMEM((2, traces, chunks * LANES), jnp.bfloat16),
        pltpu.VMEM((nx * nz * BINS, traces), jnp.bfloat16),
        pltpu.VMEM((nx * nz * BINS, traces), jnp.bfloat16),
        pltpu.VMEM((chunks, nx, nz, *cells), jnp.float32),
        pltpu.VMEM((2, 8, nz * BINS), jnp.float32),
        pltpu.VMEM((2, 2, max(nx, nz) // 2, 8, nz * BINS), jnp.float32),
        pltpu.VMEM((leads, 2, nx // 2, nz, *cells), jnp.float32),
        pltpu.VMEM((chunks - leads, 2, nz // 2, nx, *cells), jnp.float32),
        pltpu.VMEM((chunks - leads, 2, nx // 2, *cells), jnp.float32),
        pltpu.VMEM((leads, 2, nz // 2, *cells), jnp.float32),
        pltpu.VMEM((2, chunks, *cells), jnp.float32),
        pltpu.VMEM((2, chunks, 2 * IL_H * RS, LANES), jnp.float32),
        pltpu.VMEM((2, chunks, 2 * IL_H * RS, LANES), jnp.float32),
        pltpu.VMEM((chunks, *cells), jnp.float32),
        pltpu.VMEM((BINS, LANES), jnp.float32),
        pltpu.SemaphoreType.DMA((2, chunks + 1)),
        pltpu.SemaphoreType.DMA((2, chunks, 2, 2, max(nx, nz) // 2)),
        pltpu.SemaphoreType.DMA((2, 2, 2, max(nx, nz) // 2)),
        pltpu.SemaphoreType.DMA((2, 2, chunks)),
        pltpu.SemaphoreType.DMA((2, 2, chunks)),
    ]
    vmem = pl.BlockSpec(memory_space=pltpu.VMEM)
    return pl.pallas_call(
        functools.partial(stack_kernel, (chunks, nx, nz, ny)),
        out_shape=jax.ShapeDtypeStruct((2, BINS_H, chunks * LANES + 2 * EDGE), jnp.float32),
        in_specs=[vmem, vmem],
        out_specs=vmem,
        scratch_shapes=scratch,
        compiler_params=pltpu.CompilerParams(
            collective_id=0, has_side_effects=True, vmem_limit_bytes=32 << 20
        ),
        name="stack",
    )(ids, rows)


def shards(traces, fold_bins, radii):
    count = traces.shape[0]
    rows, ids = jnp.transpose(traces, (1, 0, 2)), fold_bins.reshape(1, count)
    bm = haloed_stacks(rows, ids, lax.axis_size("shot"), lax.axis_size("inline"))
    return similarity(bm, band_matrices(radii), radii)


def solution(mesh):
    placed = (P(("shot", "inline"), None, None), P(("shot", "inline"), None), P())
    return jax.shard_map(
        shards,
        mesh=mesh,
        in_specs=placed,
        out_specs=P("inline", "shot", None, None),
        check_vma=False,
    )
```

```python
import functools

import jax
import jax.numpy as jnp
from jax import lax
from jax.experimental import pallas as pl
from jax.experimental.pallas import tpu as pltpu
from jax.sharding import PartitionSpec as P

NT = 1536
LAGR = 20
NLAG = 2 * LAGR + 1
TBLK = 128
NBLK = NT // TBLK
RT_MAX = 8
RS = 2
IL_DEV = 2
XL_DEV = 8
EPS = 1e-06

IL_H = IL_DEV + 2 * RS
XL_H = XL_DEV + 2 * RS
BINS = IL_DEV * XL_DEV
BINS_H = IL_H * XL_H
OCT = 6
LANES = 128
EDGE = LANES + LANES // 2
WIDE = NT + 2 * EDGE
BAND = 288


def band_matrices(radii):
    row = jnp.arange(2)[:, None] * 8 + jnp.arange(BAND)[None, :] - 84
    offset = jnp.abs(row[None, :, :, None] - jnp.arange(TBLK)[None, None, None, :])
    weight = jnp.maximum(radii[:, None, None, None] + 1 - offset, 0)
    sample = jnp.arange(NBLK)[:, None, None] * TBLK + row[None]
    inside = (sample >= 0) & (sample < NT)
    return jnp.where(inside[..., None], weight, 0).astype(jnp.bfloat16)


def triangle(cells):
    count = len(cells)
    pair = [cells[i] + cells[i + 1] for i in range(count - 1)]
    box = [pair[i] + cells[i + 2] for i in range(count - 2)]
    pair = [box[i] + box[i + 1] for i in range(count - 3)]
    return [pair[i] + box[i + 2] for i in range(count - 4)]


def space_smooth(cell):
    columns = [triangle([cell(il, xl) for il in range(IL_H)]) for xl in range(XL_H)]
    return [triangle([columns[xl][il] for xl in range(XL_H)]) for il in range(IL_DEV)]


def split_store(ref, rows, value):
    high = value.astype(jnp.bfloat16)
    ref[0, rows, :] = high
    ref[1, rows, :] = (value - high.astype(jnp.float32)).astype(jnp.bfloat16)


def similarity_kernel(radii_ref, bm_ref, band_ref, out_ref, base, turned, lagged, smooth, bsmooth, newer, bnewer, bline, bscale):
    step = pl.program_id(0)
    place = jnp.minimum(step, NBLK)

    def tile(which, index):
        return bm_ref[which, :, pl.ds(pl.multiple_of((place + index) * LANES, LANES), LANES)]

    lane = lax.broadcasted_iota(jnp.int32, (8, LANES), 1)
    sub = lax.broadcasted_iota(jnp.int32, (8, LANES), 0)
    source = (lane + sub) % LANES
    stays = lane + sub < LANES

    def turn(row):
        return jnp.take_along_axis(jnp.broadcast_to(row, (8, LANES)), source, axis=1)

    @pl.when(step == 0)
    def _():
        for row in range(BINS_H):
            turned[row] = turn(bm_ref[1, row:row + 1, LANES:2 * LANES])

    later = tile(1, 2)
    for row in range(BINS_H):
        fresh = turn(later[row:row + 1, :])
        lagged[row] = jnp.where(stays, turned[row], fresh)
        turned[row] = fresh

    lanes = lax.broadcasted_iota(jnp.int32, (BINS_H, LANES), 1)
    for octet in range(OCT):
        shift = 8 * octet - LAGR
        if shift > 0:
            mixed = jnp.where(lanes < LANES - shift, tile(0, 1), tile(0, 0))
        else:
            mixed = jnp.where(lanes >= -shift, tile(0, 1), tile(0, 2))
        base[octet] = pltpu.roll(mixed, shift % LANES, axis=1)

    def products(octet):
        def cell(il, xl):
            row = il * XL_H + xl
            moved = lagged[row]
            if octet == OCT:
                return moved * moved
            return base[octet, row:row + 1, :] * moved
        for il, cells in enumerate(space_smooth(cell)):
            for xl in range(0, XL_DEV, 2):
                first = octet * 8 * BINS + (il * XL_DEV + xl) * 8
                split_store(newer, slice(first, first + 16), jnp.concatenate([cells[xl], cells[xl + 1]], axis=0))

    energy = [base[3, il * XL_H:(il + 1) * XL_H, :] for il in range(IL_H)]
    energy = triangle([value * value for value in energy])
    for il in range(IL_DEV):
        bline[il, :XL_H, :] = energy[il]
    parts = [triangle([bline[il, k:k + XL_DEV, :] for k in range(2 * RS + 1)])[0] for il in range(IL_DEV)]
    split_store(bnewer, slice(0, BINS), jnp.concatenate(parts, axis=0))

    eps = EPS * 81.0 * (radii_ref[jnp.clip(step - 2, 0, NBLK - 1)].astype(jnp.float32) + 1.0) ** 2

    def smoothed(parts, band):
        halves = jnp.concatenate([ref[half, rows, :] for ref, rows in parts for half in range(2)], axis=0)
        whole = jnp.dot(halves, band, preferred_element_type=jnp.float32)
        count = whole.shape[0] // (2 * len(parts))
        return [
            whole[2 * i * count:(2 * i + 1) * count] + whole[(2 * i + 1) * count:(2 * i + 2) * count]
            for i in range(len(parts))
        ]

    def band_of(octet):
        start = 40 - 8 * octet
        return band_ref[0, (start // 8) % 2, start // 16 * 16:start // 16 * 16 + 2 * LANES, :]

    bscale[...] = lax.rsqrt(smoothed([(bsmooth, slice(0, BINS))], band_of(3))[0] + eps)
    for octet in range(OCT):
        products(octet)
        band = band_of(octet)
        own_rows = slice(octet * 8 * BINS, (octet + 1) * 8 * BINS)
        energy_rows = slice(OCT * 8 * BINS, (OCT + 1) * 8 * BINS)
        cross, menergy = smoothed([(smooth, own_rows), (smooth, energy_rows)], band)
        value = cross * lax.rsqrt(menergy + eps)
        value = value.reshape(BINS, 8, LANES) * bscale[...].reshape(BINS, 1, LANES)
        count = min(8, NLAG - 8 * octet)
        for cell in range(BINS):
            il, xl = cell // XL_DEV, cell % XL_DEV
            if count == 8:
                out_ref[il, pl.ds(octet * 8 * XL_DEV + xl, 8, stride=XL_DEV), :] = value[cell]
            else:
                row = octet * 8 * XL_DEV + xl
                out_ref[il, row:row + 1, :] = value[cell, :count, :]
    products(OCT)
    for ref, fresh in ((smooth, newer), (bsmooth, bnewer)):
        ref[:, :, :LANES] = ref[:, :, LANES:]
        ref[:, :, LANES:] = fresh[...]


def similarity(bm, bands, radii):
    out = pl.pallas_call(
        similarity_kernel,
        grid=(NBLK + 2,),
        out_shape=jax.ShapeDtypeStruct((IL_DEV, NLAG * XL_DEV, NT), jnp.float32),
        in_specs=[
            pl.BlockSpec(memory_space=pltpu.SMEM),
            pl.BlockSpec((2, BINS_H, WIDE), lambda j: (0, 0, 0)),
            pl.BlockSpec((1, 2, BAND, TBLK), lambda j: (jnp.clip(j - 2, 0, NBLK - 1), 0, 0, 0)),
        ],
        out_specs=pl.BlockSpec((IL_DEV, NLAG * XL_DEV, TBLK), lambda j: (0, 0, jnp.clip(j - 2, 0, NBLK - 1))),
        scratch_shapes=[
            pltpu.VMEM((OCT, BINS_H, LANES), jnp.float32),
            pltpu.VMEM((BINS_H, 8, LANES), jnp.float32),
            pltpu.VMEM((BINS_H, 8, LANES), jnp.float32),
            pltpu.VMEM((2, (OCT + 1) * 8 * BINS, 2 * LANES), jnp.bfloat16),
            pltpu.VMEM((2, BINS, 2 * LANES), jnp.bfloat16),
            pltpu.VMEM((2, (OCT + 1) * 8 * BINS, LANES), jnp.bfloat16),
            pltpu.VMEM((2, BINS, LANES), jnp.bfloat16),
            pltpu.VMEM((IL_DEV, 16, LANES), jnp.float32),
            pltpu.VMEM((BINS, LANES), jnp.float32),
        ],
        compiler_params=pltpu.CompilerParams(vmem_limit_bytes=24 << 20),
        name="similarity",
    )(radii, bm, bands)
    return jnp.transpose(out.reshape(IL_DEV, NLAG, XL_DEV, NT), (0, 2, 1, 3))


MESH = pl.DeviceIdType.MESH
RING_X = 4
CHUNK = 2 * LANES
X_FIRST = (0, 1, 3, 5, 6, 8, 10)
ORDER = (
    0, 2, 3, 1, 4, 2, 7, 5, 9, 4, 0, 11, 8, 9, 6, 3, 7, 11, 0, 9, 1, 10, 5, 4, 7, 11, 0,
    6, 2, 4, 7, 8, 1, 3, 11, 2, 10, 4, 9, 7, 3, 5, 6, 0, 1, 8, 2, 11, 9, 3, 10, 6, 4, 1,
    5, 7, 8, 2, 3, 10, 6, 11, 1, 5, 4, 8, 0, 9, 10, 6, 3, 1, 5, 2, 8, 11, 7, 9, 10, 6, 0,
    4, 5, 1, 8, 11, 3, 10, 7, 9, 6, 0, 2, 1, 8, 4, 5, 10, 3, 11, 0, 9, 2, 8, 6, 7, 5, 10,
)


def stack_kernel(sizes, ids_ref, rows_ref, out_ref, peer_ids, peer, hot, hot_peer, part, count, count_in, x_big, z_big,
                 x_small, z_small, y_in, s_in, s_out, own, fold, pair_sem, ring_sem, count_sem, y_sem, s_sem):
    chunks, nx, nz, ny = sizes
    shot = lax.axis_index("shot")
    line = lax.axis_index("inline")
    n_shot = 2 * nx * nz
    core = shot % 2
    mx = shot // (2 * nz)
    mz = (shot // 2) % nz
    extent = {"x": nx, "z": nz}
    place = {"x": mx, "z": mz}

    def along(axis, by):
        if axis == "x":
            return ((mx + by + nx) % nx) * (2 * nz) + mz * 2 + core
        return mx * (2 * nz) + ((mz + by + nz) % nz) * 2 + core

    pair = shot + 1 - 2 * core
    partners = [(pair, line)]
    partners += [(along(axis, by), line) for axis in "xz" for by in (1, -1)]
    partners += [(shot, (line + 1) % ny), (shot, (line + ny - 1) % ny)]
    partners += [((shot + 1) % n_shot, line), ((shot + n_shot - 1) % n_shot, line)]
    barrier = pltpu.get_barrier_semaphore()
    for partner in partners:
        pl.semaphore_signal(barrier, inc=1, device_id=partner, device_id_type=MESH)

    def block_of(ref, chunk):
        return ref.at[:, :, chunk * LANES:(chunk + 1) * LANES]

    bins = nx * nz * BINS

    def one_hot(ids, target):
        def block(i, carry):
            row = lax.broadcasted_iota(jnp.int32, (32, 1), 0) + i * 32
            cell = row % BINS
            name = (row // BINS) * (2 * BINS) + core * BINS + (cell % XL_DEV) * IL_DEV + cell // XL_DEV
            target[pl.ds(pl.multiple_of(i * 32, 32), 32), :] = jnp.where(ids == name, 1.0, 0.0).astype(jnp.bfloat16)
            return carry
        lax.fori_loop(0, bins // 32, block, 0)

    one_hot(ids_ref[...], hot)
    out_ref[...] = jnp.zeros_like(out_ref)
    pl.semaphore_wait(barrier, len(partners))

    sent = []

    def send(source, target, sems, index, device, when=None):
        copy = pltpu.make_async_remote_copy(
            src_ref=source, dst_ref=target, send_sem=sems.at[(0, *index)], recv_sem=sems.at[(1, *index)],
            device_id=device, device_id_type=MESH,
        )
        if when is None:
            copy.start()
        else:
            pl.when(when)(copy.start)
        sent.append((copy, when))
        return copy

    def arrive(buffer, sems, index, when=None):
        copy = pltpu.make_async_remote_copy(
            src_ref=buffer, dst_ref=buffer, send_sem=sems.at[(0, *index)], recv_sem=sems.at[(1, *index)],
            device_id=(pair, line), device_id_type=MESH,
        )
        if when is None:
            copy.wait_recv()
        else:
            pl.when(when)(copy.wait_recv)

    def terms(ref, chunk):
        block = block_of(ref, chunk)
        return jnp.concatenate([block[0], block[1]], axis=1)

    send(ids_ref, peer_ids, pair_sem, (chunks,), (pair, line))
    for chunk in range(chunks):
        send(block_of(rows_ref, chunk), block_of(peer, chunk), pair_sem, (chunk,), (pair, line))

    @pl.when(line == 0)
    def _():
        y_in[0] = jnp.zeros_like(y_in[0])

    @pl.when(line == ny - 1)
    def _():
        y_in[1] = jnp.zeros_like(y_in[1])

    @pl.when(shot == 0)
    def _():
        s_in[0] = jnp.zeros_like(s_in[0])

    @pl.when(shot == n_shot - 1)
    def _():
        s_in[1] = jnp.zeros_like(s_in[1])

    arrive(peer_ids, pair_sem, (chunks,))
    one_hot(peer_ids[...], hot_peer)

    contract = (((1,), (1,)), ((), ()))
    ones = jnp.ones((8, hot.shape[1]), jnp.bfloat16)
    wide = nz * BINS
    sub = lax.broadcasted_iota(jnp.int32, (8, wide), 0)
    tile = jnp.zeros((8, wide), jnp.float32)
    for x in range(nx):
        counted = sum(
            lax.dot_general(ones, ref[x * wide:(x + 1) * wide, :], contract, preferred_element_type=jnp.float32)
            for ref in (hot, hot_peer)
        )
        tile = jnp.where(sub == x, counted, tile)
    count[0] = tile

    def ring(axis, sems, index, local, inbox, step, turn):
        n = extent[axis]
        hops = (n // 2, n - 1 - n // 2)
        for way in range(2):
            if step > 0 and step <= hops[way]:
                arrive(inbox(way, step - 1), sems, (*index, way, step - 1))
            if step < hops[way]:
                toward = turn if way == 0 else -turn
                dest = (place[axis] + toward * (hops[way] - step) + n) % n
                source = local(dest)
                if step > 0:
                    held = inbox(way, step - 1)
                    held[...] = held[...] + source[...]
                    source = held
                send(source, inbox(way, step), sems, (*index, way, step), (along(axis, toward), line))

    def settled(axis, inbox):
        n = extent[axis]
        return sum(inbox(way, hop - 1)[...] for way, hop in enumerate((n // 2, n - 1 - n // 2)) if hop > 0)

    first_x = [chunk for chunk in range(chunks) if chunk in X_FIRST]
    first_z = [chunk for chunk in range(chunks) if chunk not in X_FIRST]
    steps_x, steps_z = nx // 2, nz // 2

    def count_op(op):
        if op <= steps_z:
            inbox = lambda way, step: count_in.at[0, way, step]
            ring("z", count_sem, (0,), lambda dest: count.at[0], inbox, op, 1)
            if op == steps_z:
                count[1] = count[0] + settled("z", inbox)
        if op >= steps_z:
            inbox = lambda way, step: count_in.at[1, way, step]
            ring("x", count_sem, (1,), lambda dest: count.at[1], inbox, op - steps_z, 1)
            if op == steps_z + steps_x:
                total = count[1] + settled("x", inbox)
                mine = jnp.sum(jnp.where(sub == mx, total, 0.0), axis=0, keepdims=True)
                lane = lax.broadcasted_iota(jnp.int32, (BINS, wide), 1)
                cell = lax.broadcasted_iota(jnp.int32, (BINS, wide), 0)
                mine = jnp.where(lane == mz * BINS + cell, jnp.broadcast_to(mine, (BINS, wide)), 0.0)
                mine = jnp.sum(mine, axis=1, keepdims=True)
                fold[...] = jnp.broadcast_to(jnp.maximum(mine, 1.0), fold.shape)

    last = steps_x + steps_z + 2

    def chunk_op(chunk, op):
        x_leads = chunk in X_FIRST
        slot = (first_x if x_leads else first_z).index(chunk)
        turn = 1 if slot % 2 == 0 else -1
        axes = "xz" if x_leads else "zx"
        half = steps_x if x_leads else steps_z
        full = steps_x + steps_z
        big, small = (x_big, z_small) if x_leads else (z_big, x_small)
        big_in = lambda way, step: big.at[slot, way, step]
        small_in = lambda way, step: small.at[slot, way, step]
        mine = part.at[chunk, mx] if x_leads else part.at[chunk, :, mz]
        if op == 0:
            arrive(block_of(peer, chunk), pair_sem, (chunk,))
            summed = jnp.dot(hot[...], terms(rows_ref, chunk), preferred_element_type=jnp.float32) + jnp.dot(
                hot_peer[...], terms(peer, chunk), preferred_element_type=jnp.float32
            )
            part[chunk] = summed.reshape(nx, nz, BINS, CHUNK)
        if op <= half:
            local = (lambda dest: part.at[chunk, dest]) if x_leads else (lambda dest: part.at[chunk, :, dest])
            ring(axes[0], ring_sem, (chunk, 0), local, big_in, op, turn)
            if op == half:
                mine[...] = mine[...] + settled(axes[0], big_in)
        if half <= op <= full:
            local = (lambda dest: part.at[chunk, mx, dest]) if x_leads else (lambda dest: part.at[chunk, dest, mz])
            ring(axes[1], ring_sem, (chunk, 1), local, small_in, op - half, turn)
            if op == full:
                stacks = (part[chunk, mx, mz] + settled(axes[1], small_in)) / fold[:, :1]
                own[chunk] = stacks
                send(own.at[chunk], y_in.at[0, chunk], y_sem, (0, chunk), (shot, (line + 1) % ny), line < ny - 1)
                send(own.at[chunk], y_in.at[1, chunk], y_sem, (1, chunk), (shot, (line + ny - 1) % ny), line > 0)
        lanes = slice(EDGE + chunk * LANES, EDGE + (chunk + 1) * LANES)
        if op == full + 1:
            arrive(y_in.at[0, chunk], y_sem, (0, chunk), line > 0)
            arrive(y_in.at[1, chunk], y_sem, (1, chunk), line < ny - 1)
            for group, block in enumerate((y_in[0, chunk], own[chunk], y_in[1, chunk])):
                for which in range(2):
                    for il in range(IL_DEV):
                        cells = block[il * XL_DEV:(il + 1) * XL_DEV, which * LANES:(which + 1) * LANES]
                        inline = group * IL_DEV + il
                        out_ref[which, inline * XL_H + RS:inline * XL_H + RS + XL_DEV, lanes] = cells
                        edge = (which * IL_H + inline) * RS
                        s_out[0, chunk, edge:edge + RS, :] = cells[XL_DEV - RS:, :]
                        s_out[1, chunk, edge:edge + RS, :] = cells[:RS, :]
            send(s_out.at[0, chunk], s_in.at[0, chunk], s_sem, (0, chunk), ((shot + 1) % n_shot, line), shot < n_shot - 1)
            send(s_out.at[1, chunk], s_in.at[1, chunk], s_sem, (1, chunk), ((shot + n_shot - 1) % n_shot, line), shot > 0)
        if op == full + 2:
            arrive(s_in.at[0, chunk], s_sem, (0, chunk), shot > 0)
            arrive(s_in.at[1, chunk], s_sem, (1, chunk), shot < n_shot - 1)
            for side in range(2):
                for which in range(2):
                    for inline in range(IL_H):
                        edge = (which * IL_H + inline) * RS
                        row = inline * XL_H + side * (RS + XL_DEV)
                        out_ref[which, row:row + RS, lanes] = s_in[side, chunk, edge:edge + RS, :]

    done = [0] * chunks
    counted = 0
    for chunk in [chunk for chunk in ORDER if chunk < chunks]:
        op = done[chunk]
        done[chunk] += 1
        if op > last:
            continue
        if op == counted and op <= steps_x + steps_z:
            count_op(op)
            counted += 1
        chunk_op(chunk, op)

    for copy, when in sent:
        if when is None:
            copy.wait_send()
        else:
            pl.when(when)(copy.wait_send)


def haloed_stacks(rows, ids, n_shot, ny, nx=RING_X):
    traces, chunks = rows.shape[1], rows.shape[2] // LANES
    nz = n_shot // (2 * nx)
    leads = len([chunk for chunk in range(chunks) if chunk in X_FIRST])
    cells = (BINS, CHUNK)
    scratch = [
        pltpu.VMEM((1, traces), jnp.int32),
        pltpu.VMEM((2, traces, chunks * LANES), jnp.bfloat16),
        pltpu.VMEM((nx * nz * BINS, traces), jnp.bfloat16),
        pltpu.VMEM((nx * nz * BINS, traces), jnp.bfloat16),
        pltpu.VMEM((chunks, nx, nz, *cells), jnp.float32),
        pltpu.VMEM((2, 8, nz * BINS), jnp.float32),
        pltpu.VMEM((2, 2, max(nx, nz) // 2, 8, nz * BINS), jnp.float32),
        pltpu.VMEM((leads, 2, nx // 2, nz, *cells), jnp.float32),
        pltpu.VMEM((chunks - leads, 2, nz // 2, nx, *cells), jnp.float32),
        pltpu.VMEM((chunks - leads, 2, nx // 2, *cells), jnp.float32),
        pltpu.VMEM((leads, 2, nz // 2, *cells), jnp.float32),
        pltpu.VMEM((2, chunks, *cells), jnp.float32),
        pltpu.VMEM((2, chunks, 2 * IL_H * RS, LANES), jnp.float32),
        pltpu.VMEM((2, chunks, 2 * IL_H * RS, LANES), jnp.float32),
        pltpu.VMEM((chunks, *cells), jnp.float32),
        pltpu.VMEM((BINS, LANES), jnp.float32),
        pltpu.SemaphoreType.DMA((2, chunks + 1)),
        pltpu.SemaphoreType.DMA((2, chunks, 2, 2, max(nx, nz) // 2)),
        pltpu.SemaphoreType.DMA((2, 2, 2, max(nx, nz) // 2)),
        pltpu.SemaphoreType.DMA((2, 2, chunks)),
        pltpu.SemaphoreType.DMA((2, 2, chunks)),
    ]
    vmem = pl.BlockSpec(memory_space=pltpu.VMEM)
    return pl.pallas_call(
        functools.partial(stack_kernel, (chunks, nx, nz, ny)),
        out_shape=jax.ShapeDtypeStruct((2, BINS_H, chunks * LANES + 2 * EDGE), jnp.float32),
        in_specs=[vmem, vmem],
        out_specs=vmem,
        scratch_shapes=scratch,
        compiler_params=pltpu.CompilerParams(
            collective_id=0, has_side_effects=True, vmem_limit_bytes=32 << 20
        ),
        name="stack",
    )(ids, rows)


def shards(traces, fold_bins, radii):
    count = traces.shape[0]
    rows, ids = jnp.transpose(traces, (1, 0, 2)), fold_bins.reshape(1, count)
    bm = haloed_stacks(rows, ids, lax.axis_size("shot"), lax.axis_size("inline"))
    return similarity(bm, band_matrices(radii), radii)


def solution(mesh):
    placed = (P(("shot", "inline"), None, None), P(("shot", "inline"), None), P())
    return jax.shard_map(
        shards,
        mesh=mesh,
        in_specs=placed,
        out_specs=P("inline", "shot", None, None),
        check_vma=False,
    )
```
